32 devices in a mesh: grp: 4 (over z), sub: 8 (over y, x, core).
Axes of the slice: x: 2, y: 2, z: 4, core: 2. Of those that a mesh axis runs over, the one named last changes fastest.
Arguments:
- leaf_bases: bfloat16 [384, 256, 128], P(('grp', 'sub')), may hold values from -6 to 6
- leaf_transfers: bfloat16 [384, 128, 128], P(('grp', 'sub')), may hold values from -1 to 2
- leaf_blocks: bfloat16 [384, 6, 128, 128], P(('grp', 'sub')), may hold values from -6 to 6
- leaf_partner_dev: int32 [384, 6], P(('grp', 'sub')), may hold values from 0 to 7, all different within a row; in each aligned block of 12 rows (0 to 11, 12 to 23, ...) at most 12 rows name the same one
- leaf_partner_slot: int32 [384, 6], P(('grp', 'sub')), may hold values from 0 to 11
- parent_blocks: bfloat16 [192, 3, 128, 128], P(('grp', 'sub')), may hold values from -6 to 6
- parent_partner_group: int32 [192, 3], P(('grp', 'sub')), may hold values from 0 to 3, all different within a row; in each aligned block of 6 rows (0 to 5, 6 to 11, ...) at most 6 rows name the same one
- parent_partner_slot: int32 [192, 3], P(('grp', 'sub')), may hold values from 0 to 5
- leaf_start: float32 [64, 128], replicated, may hold values from -6 to 6
- parent_start: float32 [64, 128], replicated, may hold values from -6 to 6
Outputs:
- new_leaf_bases: bfloat16 [384, 64, 256], P(('grp', 'sub'))
- new_leaf_blocks: bfloat16 [384, 6, 4096], P(('grp', 'sub'))
- new_parent_blocks: bfloat16 [192, 3, 4096], P(('grp', 'sub'))
The draws below stay inside these ranges and needn't reach their ends.
Inputs may be any that keep to these rules, and one draw needn't show every extreme that they name: `leaf_partner_dev`: one leaf's partners lie on different devices of its group; among the leaves of one device no index appears more than 12 times, and that count is reached on some device. `parent_partner_group`: one parent's partners lie in different groups; among the parents of one device no group appears more than 6 times, and that count is reached on some device.
All inputs are finite; a program needn't handle non-finite values.
Results may differ from the reference program's by a relative error of at most 0.033.
Values may be sent and summed in bfloat16 or wider, within the bound.
No kernel may reach another device: no remote copies, remote signals or barrier semaphores. Data moves between devices by JAX's collectives and lax.ppermute only.
A program may use at most 64 MiB of HBM per device.

```python
import math
import jax
import jax.numpy as jnp
import numpy as np
from jax import lax

K = 128
R = 64
LEAF_DEV = 12
LEAF_ROWS = 256
NC_IN = 6
NC_X = 3
PAR_DEV = 6
NLEAF = 384
NPAR = 192
CAP_IN = 12
CAP_X = 6
N_GRP = 4
N_SUB = 8


def draw_leaf_transfers(key, part):
    noise = jnp.clip(jax.random.normal(key, (NLEAF, K, K), jnp.float32), -4.0, 4.0)
    identity = jnp.eye(K, dtype=jnp.float32)[None, :, :]
    return (identity + 0.5 * noise / math.sqrt(K)).astype(jnp.bfloat16)


def place_ends(values, own_key, least, largest):
    extent = values.shape
    spot = [jax.random.randint(jax.random.fold_in(own_key, axis), (), 0, extent[axis]) for axis in range(len(extent))]
    values = values.at[tuple(spot)].set(least)
    longest = extent.index(max(extent))
    spot[longest] = (spot[longest] + 1) % extent[longest]
    return values.at[tuple(spot)].set(largest)


def level_of(stream_key, shape, cuts, low, largest):
    gain, own = 1.0, jax.random.fold_in(stream_key, 6)
    for axis_at, shards_of in cuts:
        heights = jnp.exp(jax.random.uniform(jax.random.fold_in(own, axis_at), (shards_of,), jnp.float32, low / len(cuts), largest / len(cuts)))
        gain = gain * jnp.repeat(heights, shape[axis_at] // shards_of).reshape([-1 if axis == axis_at else 1 for axis in range(len(shape))])
    return gain


def routed_block(own_key, own, number, rows, number_of, top, bound, lean):
    order = jax.random.permutation(own_key, number_of)
    packed, ordinary = shares(number_of, rows * top, bound, lean, True), shares(number_of, rows * top, bound, lean, False)
    places = jnp.arange(number_of)

    def named(lengths, turn):
        used = int((lengths > 0).sum())
        fixed = max(1, used // 4)
        shifted = fixed + (places - fixed + turn * (used - fixed)) % max(1, number_of - fixed)
        return jnp.zeros((number_of,), jnp.int32).at[order[jnp.where(places < fixed, places, shifted)]].set(jnp.asarray(lengths, jnp.int32))

    lengths = jnp.where(number % 4 == 0, named(packed, number // 4), named(ordinary, number - number // 4 - 1))
    mixed = jax.random.permutation(jax.random.fold_in(own, 3), number_of)
    donor, taker = mixed[0:number_of // 2 * 2:2], mixed[1:number_of // 2 * 2:2]
    slack = jnp.minimum(lengths[donor] - 1, bound - lengths[taker]) // 2
    slack = jnp.where((donor == order[0]) | (taker == order[0]) | (lengths[taker] == 0), 0, jnp.maximum(slack, 0))
    shifted = jax.random.randint(jax.random.fold_in(own, 4), (number_of // 2,), 0, 1 << 20) % (slack + 1)
    lengths = lengths.at[donor].add(-shifted).at[taker].add(shifted)
    items = jnp.searchsorted(jnp.cumsum(lengths), jnp.arange(rows * top), side="right").astype(jnp.int32)
    grid = items.reshape(top, rows).T
    grid = grid[jax.random.permutation(jax.random.fold_in(own, 1), rows)]
    turn = jax.random.randint(jax.random.fold_in(own, 2), (rows, 1), 0, top)
    return jnp.take_along_axis(grid, (jnp.arange(top)[None, :] + turn) % top, axis=1)


def shares(amount, total, bound, skew, full):
    loads = [(1 << 20) // math.isqrt(standing ** skew) + 1 for standing in range(1, amount + 1)]
    largest = bound if full else min(bound, max(-(-total // amount), total * loads[0] // sum(loads)))
    least = 1 if total - largest >= amount - 1 else 0
    counts, surplus = [largest] + [least] * (amount - 1), total - largest - least * (amount - 1)
    while surplus > 0:
        candidates = [i for i in range(1, amount) if counts[i] < largest] or [i for i in range(1, amount) if counts[i] < bound]
        mass, budget = sum([loads[i] for i in candidates]), surplus
        for i in candidates:
            addition = min(bound - counts[i], max(1, budget * loads[i] // mass), surplus)
            counts[i] = counts[i] + addition
            surplus = surplus - addition
    return np.array(counts)


def bell_draw(stream_key, extent, spread, most, cuts=(), held_as=jnp.bfloat16):
    result = jax.random.normal(stream_key, extent, jnp.float32) * spread
    if len(cuts) > 0:
        result = level_of(stream_key, extent, cuts, -0.22, 0.18) * result
    return jnp.clip(result, min=-most, max=most).astype(held_as)


def setup_inputs(seed: int = 0) -> dict:
    splits = jax.random.split(jax.random.key(seed), 11)
    leaf_bases = bell_draw(splits[0], (NLEAF, LEAF_ROWS, K), 1.0, 6.0, ((0, 32),))
    leaf_transfers = draw_leaf_transfers(jax.random.fold_in(splits[10], 71), 0)
    leaf_blocks = bell_draw(splits[2], (NLEAF, NC_IN, K, K), 1.0, 6.0, ((0, 32),))
    leaf_partner_dev_keys = jax.random.split(jax.random.fold_in(splits[3], 1), NLEAF // LEAF_DEV)
    leaf_partner_dev_turns = jax.random.permutation(jax.random.fold_in(splits[3], 3), NLEAF // LEAF_DEV)
    leaf_partner_dev = jax.vmap(lambda own, number: routed_block(jax.random.fold_in(splits[3], 2), own, number, LEAF_DEV, N_SUB, NC_IN, CAP_IN, 2))(leaf_partner_dev_keys, leaf_partner_dev_turns).reshape((NLEAF, NC_IN))
    leaf_partner_slot = place_ends(jax.random.randint(splits[4], (NLEAF, NC_IN), 0, LEAF_DEV), jax.random.fold_in(splits[4], 1), 0, LEAF_DEV - 1).astype(jnp.int32)
    parent_blocks = bell_draw(splits[5], (NPAR, NC_X, K, K), 1.0, 6.0, ((0, 32),))
    parent_partner_group_keys = jax.random.split(jax.random.fold_in(splits[6], 1), NPAR // PAR_DEV)
    parent_partner_group_turns = jax.random.permutation(jax.random.fold_in(splits[6], 3), NPAR // PAR_DEV)
    parent_partner_group = jax.vmap(lambda own, number: routed_block(jax.random.fold_in(splits[6], 2), own, number, PAR_DEV, N_GRP, NC_X, CAP_X, 2))(parent_partner_group_keys, parent_partner_group_turns).reshape((NPAR, NC_X))
    parent_partner_slot = place_ends(jax.random.randint(splits[7], (NPAR, NC_X), 0, PAR_DEV), jax.random.fold_in(splits[7], 1), 0, PAR_DEV - 1).astype(jnp.int32)
    leaf_start = bell_draw(splits[8], (R, K), 1.0, 6.0, (), jnp.float32)
    parent_start = bell_draw(splits[9], (R, 2 * R), 1.0, 6.0, (), jnp.float32)
    return {"leaf_bases": leaf_bases, "leaf_transfers": leaf_transfers, "leaf_blocks": leaf_blocks, "leaf_partner_dev": leaf_partner_dev, "leaf_partner_slot": leaf_partner_slot, "parent_blocks": parent_blocks, "parent_partner_group": parent_partner_group, "parent_partner_slot": parent_partner_slot, "leaf_start": leaf_start, "parent_start": parent_start}


TOP_PRECISION = lax.Precision.HIGHEST

def single(values):
    return values.astype(jnp.float32)

def subspace(weight, start_rows):
    basis_rows = jnp.broadcast_to(start_rows, (weight.shape[0],) + start_rows.shape)
    image_rows = jnp.einsum('brn,bnm->brm', basis_rows, weight, precision=TOP_PRECISION)
    image_rows = jnp.einsum('brn,bnm->brm', image_rows, weight, precision=TOP_PRECISION)
    cross_gram = jnp.einsum('brn,bsn->brs', image_rows, image_rows, precision=TOP_PRECISION)
    factor = jnp.linalg.cholesky(cross_gram)
    return jax.scipy.linalg.solve_triangular(factor, image_rows, lower=True)

def reference(leaf_bases, leaf_transfers, leaf_blocks, leaf_partner_dev, leaf_partner_slot, parent_blocks, parent_partner_group, parent_partner_slot, leaf_start, parent_start):
    devices_all = N_GRP * N_SUB
    device_ids = jnp.arange(devices_all, dtype=jnp.int32)
    leaf_slots = jnp.arange(LEAF_DEV, dtype=jnp.int32)
    parent_slots = jnp.arange(PAR_DEV, dtype=jnp.int32)

    def parent_section_one(device):
        blocks = single(lax.dynamic_slice_in_dim(parent_blocks, device * PAR_DEV, PAR_DEV, 0))
        return jnp.einsum('pckl,pcml->pkm', blocks, blocks, precision=TOP_PRECISION)
    parent_weight = lax.map(parent_section_one, device_ids).reshape(NPAR, K, K)

    def leaf_section(device):
        pair_offset = device // 2 * 2
        owners = (pair_offset + leaf_slots // PAR_DEV) * PAR_DEV + leaf_slots % PAR_DEV
        descended = parent_weight[owners]
        transfers = single(lax.dynamic_slice_in_dim(leaf_transfers, device * LEAF_DEV, LEAF_DEV, 0))
        blocks = single(lax.dynamic_slice_in_dim(leaf_blocks, device * LEAF_DEV, LEAF_DEV, 0))
        weight = jnp.einsum('jckl,jcml->jkm', blocks, blocks, precision=TOP_PRECISION)
        carried = jnp.einsum('jka,jab->jkb', transfers, descended, precision=TOP_PRECISION)
        weight = weight + jnp.einsum('jkb,jmb->jkm', carried, transfers, precision=TOP_PRECISION)
        change = lax.optimization_barrier(subspace(weight, leaf_start).astype(jnp.bfloat16))
        projected = jnp.einsum('jrk,jkm->jrm', single(change), transfers, precision=TOP_PRECISION)
        bases = single(lax.dynamic_slice_in_dim(leaf_bases, device * LEAF_DEV, LEAF_DEV, 0))
        new_bases = jnp.einsum('jrk,jnk->jrn', single(change), bases, precision=TOP_PRECISION).astype(jnp.bfloat16)
        return (change, projected, new_bases)
    change_all, projected_all, new_leaf_bases = lax.map(leaf_section, device_ids)
    change_all = change_all.reshape(NLEAF, R, K)
    projected_all = projected_all.reshape(NLEAF, R, K)
    new_leaf_bases = new_leaf_bases.reshape(NLEAF, R, LEAF_ROWS)

    def parent_section_two(device):
        pair_offset = device // 2 * 2
        column = device % 2 * PAR_DEV + parent_slots
        first_child = projected_all[pair_offset * LEAF_DEV + column]
        second_child = projected_all[(pair_offset + 1) * LEAF_DEV + column]
        stacked = jnp.concatenate([first_child, second_child], axis=1)
        weight = lax.dynamic_slice_in_dim(parent_weight, device * PAR_DEV, PAR_DEV, 0)
        parent_left = jnp.einsum('prk,pkm->prm', stacked, weight, precision=TOP_PRECISION)
        parent_gram = jnp.einsum('prm,psm->prs', parent_left, stacked, precision=TOP_PRECISION)
        parent_rows = subspace(parent_gram, parent_start)
        return jnp.einsum('prs,psk->prk', parent_rows, stacked, precision=TOP_PRECISION).astype(jnp.bfloat16)
    parent_change = lax.optimization_barrier(lax.map(parent_section_two, device_ids).reshape(NPAR, R, K))

    def couple_leaves(device):
        group_base = device // N_SUB * N_SUB
        dev_rows = lax.dynamic_slice_in_dim(leaf_partner_dev, device * LEAF_DEV, LEAF_DEV, 0)
        slot_rows = lax.dynamic_slice_in_dim(leaf_partner_slot, device * LEAF_DEV, LEAF_DEV, 0)
        partner = (group_base + dev_rows) * LEAF_DEV + slot_rows
        distant_site = single(change_all[partner])
        own_rows = single(lax.dynamic_slice_in_dim(change_all, device * LEAF_DEV, LEAF_DEV, 0))
        blocks = single(lax.dynamic_slice_in_dim(leaf_blocks, device * LEAF_DEV, LEAF_DEV, 0))
        leaf_midpoint = jnp.einsum('jrk,jckl->jcrl', own_rows, blocks, precision=TOP_PRECISION).astype(jnp.bfloat16)
        leaf_midpoint = single(lax.optimization_barrier(leaf_midpoint))
        final_output = jnp.einsum('jcrl,jcsl->jcrs', leaf_midpoint, distant_site, precision=TOP_PRECISION).astype(jnp.bfloat16)
        return final_output.reshape(LEAF_DEV, NC_IN, R * R)
    new_leaf_blocks = lax.map(couple_leaves, device_ids).reshape(NLEAF, NC_IN, R * R)

    def couple_parents(device):
        inner_index = device % N_SUB
        group_rows = lax.dynamic_slice_in_dim(parent_partner_group, device * PAR_DEV, PAR_DEV, 0)
        slot_rows = lax.dynamic_slice_in_dim(parent_partner_slot, device * PAR_DEV, PAR_DEV, 0)
        partner = (group_rows * N_SUB + inner_index) * PAR_DEV + slot_rows
        distant_site = single(parent_change[partner])
        own_rows = single(lax.dynamic_slice_in_dim(parent_change, device * PAR_DEV, PAR_DEV, 0))
        blocks = single(lax.dynamic_slice_in_dim(parent_blocks, device * PAR_DEV, PAR_DEV, 0))
        parent_midpoint = jnp.einsum('prk,pckl->pcrl', own_rows, blocks, precision=TOP_PRECISION).astype(jnp.bfloat16)
        parent_midpoint = single(lax.optimization_barrier(parent_midpoint))
        final_output = jnp.einsum('juog,juqg->juoq', parent_midpoint, distant_site, precision=TOP_PRECISION).astype(jnp.bfloat16)
        return final_output.reshape(PAR_DEV, NC_X, R * R)
    new_parent_blocks = lax.map(couple_parents, device_ids).reshape(NPAR, NC_X, R * R)
    return (new_leaf_bases, new_leaf_blocks, new_parent_blocks)
```

```python
import jax
import jax.numpy as jnp
from jax import lax
from jax.experimental import pallas as pl
from jax.experimental.pallas import tpu as pltpu
from jax.sharding import PartitionSpec as P

F32 = jnp.float32
BF16 = jnp.bfloat16
PIVOTS = 4
MIB = 1 << 20


def cat(parts, axis):
    return jnp.concatenate(parts, axis=axis)


def halves(value):
    high = value.astype(BF16)
    low = (value - high.astype(F32)).astype(BF16)
    return high, low


def dot(left, right):
    return lax.dot_general(left, right, (((1,), (0,)), ((), ())), preferred_element_type=F32)


def dot_t(left, right):
    return lax.dot_general(left, right, (((1,), (1,)), ((), ())), preferred_element_type=F32)


def fold(value):
    width = value.shape[1] // 2
    return value[:, :width] + value[:, width:]


def wide(value):
    return cat(halves(value), 1)


def tall(value):
    both = wide(value)
    return cat([both, both], 0)


def gram_sum(parts):
    row = cat(parts, 1)
    return dot_t(row, row)


def eliminate(grid, made, rank):
    shape = (8, 128)
    lane = lax.broadcasted_iota(jnp.int32, shape, 1)
    half = jnp.where(lane < rank, 0, rank)
    local = lane - half

    def spread(value, column):
        return jnp.take_along_axis(value, half + column, axis=1)

    for first in range(0, rank, PIVOTS):
        last = first + PIVOTS
        rows = [grid[8 * i : 8 * i + 8, :] for i in range(first, last)]
        corner = [[None] * PIVOTS for _ in range(PIVOTS)]
        for p in range(PIVOTS):
            for q in range(p, PIVOTS):
                corner[p][q] = spread(rows[p], first + q)
        inside = (local >= first) & (local < last)
        rows = [
            jnp.where(inside, (local == first + p).astype(F32), rows[p]) for p in range(PIVOTS)
        ]
        inverse = []
        for p in range(PIVOTS):
            inverse.append(1.0 / corner[p][p])
            for q in range(p + 1, PIVOTS):
                factor = corner[p][q] * inverse[p]
                for s in range(q, PIVOTS):
                    corner[q][s] = corner[q][s] - factor * corner[p][s]
                rows[q] = rows[q] - factor * rows[p]
        scaled = [rows[p] * inverse[p] for p in range(PIVOTS)]
        for i in range(last, rank):
            row = jnp.where(inside, 0.0, grid[8 * i : 8 * i + 8, :])
            for p in range(PIVOTS):
                row = row - spread(scaled[p], i) * rows[p]
            grid[8 * i : 8 * i + 8, :] = row
        for p in range(PIVOTS):
            i = first + p
            done = jnp.where(local < last, rows[p] * lax.rsqrt(corner[p][p]), 0.0)
            made[8 * i : 8 * i + 8, :] = done


def pair_rows(made, stored, pair, rank):
    wide_rank = 2 * rank
    factor = wide(made[pl.ds(pair, rank, stride=8), :])
    both = stored[pair]
    zero = jnp.zeros((rank, both.shape[1]), F32)
    spread = cat([cat([both[:rank], zero], 1), cat([zero, both[rank:]], 1)], 0)
    high, low = halves(spread)
    return dot(factor, cat([high, high], 0)) + dot(factor, cat([low, low], 0))


def store_gram(grid, stored, pair, images, rank):
    both = cat(images, 0)
    stored[pair] = both
    both_wide = wide(both)
    high, low = halves(both)
    full = dot_t(both_wide, cat([cat([high, high], 1), cat([low, low], 1)], 0))
    full = fold(full)
    lane = lax.broadcasted_iota(jnp.int32, (rank, 2 * rank), 1)
    grid[pl.ds(pair, rank, stride=8), :] = jnp.where(lane < rank, full[:rank], full[rank:])


def sent_weights(blocks, weight, held, sems):
    half = weight.shape[0]
    links = blocks.shape[1]
    start = (1 - lax.axis_index("sub") % 2) * half
    copies = [
        pltpu.make_async_copy(blocks.at[start + j], held.at[j], sems.at[j]) for j in range(half)
    ]
    for copy in copies:
        copy.start()
    for j in range(half):
        copies[j].wait()
        weight[j] = gram_sum([held[j, c] for c in range(links)])


def kept_weights(blocks, parents, weight, parent_weight, held, held_parents, sems):
    half = weight.shape[0]
    links = blocks.shape[1]
    start = (lax.axis_index("sub") % 2) * half
    copies = [
        pltpu.make_async_copy(blocks.at[start + j], held.at[j], sems.at[j]) for j in range(half)
    ] + [
        pltpu.make_async_copy(parents.at[j], held_parents.at[j], sems.at[half + j])
        for j in range(half)
    ]
    for copy in copies:
        copy.start()
    for j in range(half):
        copies[j].wait()
        weight[j] = gram_sum([held[j, c] for c in range(links)])
    for j in range(half):
        copies[half + j].wait()
        parent_weight[j] = gram_sum([held_parents[j, c] for c in range(parents.shape[1])])


def leaf_step(own, other, parent, transfers, other_transfers, start, change, stacked, grid, made, stored):
    rank = start.shape[0]
    half = own.shape[0]
    member = lax.axis_index("sub") % 2
    start_wide = wide(start[...])
    for j in range(half):
        own_move = transfers[member * half + j]
        other_move = other_transfers[j]
        carried = fold(dot(cat([own_move, other_move], 0), wide(parent[j])))
        images = []
        size = own_move.shape[0]
        for at, (move, weight) in enumerate(((own_move, own), (other_move, other))):
            full = weight[j] + dot_t(
                wide(carried[at * size : at * size + size]), cat([move, move], 1)
            )
            folded = tall(full)
            image = fold(dot(start_wide, folded))
            images.append(fold(dot(wide(image), folded)))
        store_gram(grid, stored, j, images, rank)
    eliminate(grid, made, rank)
    for j in range(half):
        found = pair_rows(made, stored, j, rank).astype(BF16)
        width = found.shape[1] // 2
        mine, theirs = found[:, :width], found[:, width:]
        change[0, j] = mine
        change[1, j] = theirs
        stacked[j, member] = dot(mine, transfers[member * half + j])
        stacked[j, 1 - member] = dot(theirs, other_transfers[j])


def parent_step(parent, stacked, start, change, grid, made, stored):
    rank = start.shape[0]
    half = parent.shape[0]
    start_wide = wide(start[...])
    for pair in range(half // 2):
        images = []
        for j in (2 * pair, 2 * pair + 1):
            rows = cat([stacked[j, 0], stacked[j, 1]], 0)
            rows_wide = wide(rows)
            high, low = halves(rows)
            left = fold(dot(rows_wide, tall(parent[j])))
            gram = fold(
                dot_t(wide(left), cat([cat([high, high], 1), cat([low, low], 1)], 0))
            )
            folded = tall(gram)
            image = fold(dot(start_wide, folded))
            images.append(fold(dot(wide(image), folded)))
        store_gram(grid, stored, pair, images, rank)
    eliminate(grid, made, rank)
    for pair in range(half // 2):
        found = pair_rows(made, stored, pair, rank)
        width = found.shape[1] // 2
        for at in range(2):
            j = 2 * pair + at
            rows = cat([stacked[j, 0], stacked[j, 1]], 0)
            mixed = wide(found[:, at * width : at * width + width])
            change[j] = fold(dot(mixed, tall(rows))).astype(BF16)


def parted(value, scratch):
    scratch[...] = value.astype(F32)
    count = value.shape[0] // 2
    return cat(
        [scratch[pl.ds(0, count, stride=2), :], scratch[pl.ds(1, count, stride=2), :]], 0
    ).astype(BF16)


def middle_step(
    change, swapped, parent_change, bases, blocks, parents,
    new_bases, leaf_half, parent_half,
    held_bases, held, held_parents, order, sems,
):
    half = change.shape[1]
    count, links = blocks.shape[0], blocks.shape[1]
    member = lax.axis_index("sub") % 2
    where = [member * half + j for j in range(half)] + [(1 - member) * half + j for j in range(half)]
    copies = []
    for at in range(count):
        copies.append(
            (
                pltpu.make_async_copy(bases.at[where[at]], held_bases.at[at], sems.at[2 * at]),
                pltpu.make_async_copy(blocks.at[where[at]], held.at[at], sems.at[2 * at + 1]),
            )
        )
    whole = pltpu.make_async_copy(parents, held_parents, sems.at[2 * count])
    for first, second in copies:
        first.start()
        second.start()
    whole.start()
    for at in range(count):
        rows = change[0, at] if at < half else swapped[1, at - half]
        ordered = parted(rows, order.at[at % 2])
        copies[at][0].wait()
        new_bases[where[at]] = dot_t(rows, held_bases[at]).astype(BF16)
        copies[at][1].wait()
        leaf_half[where[at]] = dot(ordered, cat([held[at, c] for c in range(links)], 1)).astype(BF16)
    whole.wait()
    for j in range(half):
        ordered = parted(parent_change[j], order.at[j % 2])
        parent_half[j] = dot(
            ordered, cat([held_parents[j, c] for c in range(parents.shape[1])], 1)
        ).astype(BF16)


def couple(middle, partner, lanes_low):
    full = dot_t(middle, cat([partner, partner], 0))
    count = full.shape[0] // 2
    return jnp.where(lanes_low, full[:count], full[count:])


def write_rows(out, at, order, links, count):
    for m in range(count):
        out[at, :, m * 128 : m * 128 + 128] = order[8 * m : 8 * m + links, :].astype(BF16)


def leaf_couple(devs, slots, middle, *rest):
    chips = (len(rest) - 4) // 2
    near, far = rest[:chips], rest[chips : 2 * chips]
    out, held, order, sems = rest[2 * chips :]
    count, links = out.shape[0], out.shape[1]
    half = count // 2
    rank = middle.shape[1]
    index = lax.axis_index("sub")
    member, chip = index % 2, index // 2
    copies = []
    for m in range(chips):
        for side, source in ((0, near[m]), (1, far[m])):
            copies.append(
                pltpu.make_async_copy(source, held.at[2 * m + side], sems.at[2 * m + side])
            )
    for copy in copies:
        copy.start()
    for copy in copies:
        copy.wait()
    low = lax.broadcasted_iota(jnp.int32, (rank // 2, 2 * rank), 1) < rank

    @pl.loop(0, count)
    def _(t):
        for c in range(links):
            dev, slot = devs[t, c], slots[t, c]
            side = jnp.where(slot >= half, 1, 0)
            place = slot - side * half
            box = ((dev // 2) ^ chip) * 2 + (side ^ member)
            partner = held[box, (dev % 2) ^ side, place]
            order[pl.ds(c, rank // 2, stride=8), :] = couple(
                middle[t, :, c * 128 : c * 128 + 128], partner, low
            )
        write_rows(out, t, order, links, rank // 2)


def parent_couple(groups, slots, middle, *rest):
    boxes = len(rest) - 2
    held = rest[:boxes]
    out, order = rest[boxes:]
    count, links = out.shape[0], out.shape[1]
    rank = middle.shape[1]
    mine = lax.axis_index("grp")
    low = lax.broadcasted_iota(jnp.int32, (rank // 2, 2 * rank), 1) < rank
    for p in range(count):
        for c in range(links):
            box = groups[p, c] ^ mine
            slot = slots[p, c]
            partner = held[0][slot]
            for m in range(1, boxes):
                partner = jnp.where(box == m, held[m][slot], partner)
            order[p % 2, pl.ds(c, rank // 2, stride=8), :] = couple(
                middle[p, :, c * 128 : c * 128 + 128], partner, low
            )
        write_rows(out, p, order.at[p % 2], links, rank // 2)


VMEM = pl.BlockSpec(memory_space=pltpu.VMEM)
ANY = pl.BlockSpec(memory_space=pl.ANY)
SMEM = pl.BlockSpec(memory_space=pltpu.SMEM)


def call(body, ins, out_shapes, scratch, name, mib, flops, moved):
    many = isinstance(out_shapes, list)
    return pl.pallas_call(
        body,
        out_shape=out_shapes,
        in_specs=ins,
        out_specs=[VMEM] * len(out_shapes) if many else VMEM,
        scratch_shapes=scratch,
        name=name,
        compiler_params=pltpu.CompilerParams(vmem_limit_bytes=mib * MIB),
        cost_estimate=pl.CostEstimate(flops=flops, bytes_accessed=moved, transcendentals=0),
    )


def swap(block, axis, mask):
    count = lax.axis_size(axis)
    return lax.ppermute(block, axis, [(i, i ^ mask) for i in range(count)])


def shards(
    leaf_bases,
    leaf_transfers,
    leaf_blocks,
    leaf_partner_dev,
    leaf_partner_slot,
    parent_blocks,
    parent_partner_group,
    parent_partner_slot,
    leaf_start,
    parent_start,
):
    count, links, old = leaf_blocks.shape[:3]
    half, parent_links = parent_blocks.shape[:2]
    rank = leaf_start.shape[0]
    points = leaf_bases.shape[1]
    chips = lax.axis_size("sub") // 2
    groups = lax.axis_size("grp")
    member = lax.axis_index("sub") % 2
    shape = jax.ShapeDtypeStruct
    dma = pltpu.SemaphoreType.DMA
    square = half * old * old

    moved = lax.dynamic_slice_in_dim(leaf_transfers, (1 - member) * half, half, 0)
    other_transfers = swap(moved, "sub", 1)
    sent = call(
        sent_weights, [ANY], shape((half, old, old), F32),
        [pltpu.VMEM((half, links, old, old), BF16), dma((half,))],
        "sent_weights", 8, 2 * links * square * old, 2 * links * square,
    )(leaf_blocks)
    other = swap(sent, "sub", 1)
    own, parent_weight = call(
        kept_weights, [ANY, ANY], [shape((half, old, old), F32), shape((half, old, old), F32)],
        [
            pltpu.VMEM((half, links, old, old), BF16),
            pltpu.VMEM((half, parent_links, old, old), BF16),
            dma((2 * half,)),
        ],
        "kept_weights", 12, 2 * (links + parent_links) * square * old, 8 * links * square,
    )(leaf_blocks, parent_blocks)
    tables = [
        pltpu.VMEM((8 * rank, 2 * rank), F32),
        pltpu.VMEM((8 * rank, 2 * rank), F32),
        pltpu.VMEM((half, 2 * rank, old), F32),
    ]
    change, stacked = call(
        leaf_step, [VMEM] * 6,
        [shape((2, half, rank, old), BF16), shape((half, 2, rank, old), F32)],
        tables, "leaf_step", 12, 40 * square * old, 8 * square,
    )(own, other, parent_weight, leaf_transfers, other_transfers, leaf_start)

    near = [change]
    far = [swap(change, "sub", 1)]
    for m in range(1, chips):
        near.append(swap(change, "sub", 2 * m))
    parent_change = call(
        parent_step, [VMEM] * 3, shape((half, rank, old), BF16),
        tables, "parent_step", 12, 20 * square * old, 8 * square,
    )(parent_weight, stacked, parent_start)
    for m in range(1, chips):
        far.append(swap(near[m], "sub", 1))
    parents_held = [parent_change]
    for m in range(1, groups):
        parents_held.append(swap(parent_change, "grp", m))
    new_leaf_bases, leaf_half, parent_half = call(
        middle_step, [VMEM] * 3 + [ANY] * 3,
        [
            shape((count, rank, points), BF16),
            shape((count, rank, links * old), BF16),
            shape((half, rank, parent_links * old), BF16),
        ],
        [
            pltpu.VMEM((count, points, old), BF16),
            pltpu.VMEM((count, links, old, old), BF16),
            pltpu.VMEM((half, parent_links, old, old), BF16),
            pltpu.VMEM((2, rank, old), F32),
            dma((2 * count + 1,)),
        ],
        "middle_step", 16, 20 * square * old, 12 * links * square,
    )(change, far[0], parent_change, leaf_bases, leaf_blocks, parent_blocks)
    new_leaf_blocks = call(
        leaf_couple, [SMEM, SMEM, VMEM] + [ANY] * (2 * chips),
        shape((count, links, rank * rank), BF16),
        [
            pltpu.VMEM((2 * chips, 2, half, rank, old), BF16),
            pltpu.VMEM((4 * rank, 2 * rank), F32),
            dma((2 * chips,)),
        ],
        "leaf_couple", 16, 12 * square * old, 12 * square,
    )(leaf_partner_dev, leaf_partner_slot, leaf_half, *near, *far)
    new_parent_blocks = call(
        parent_couple, [SMEM, SMEM, VMEM] + [VMEM] * groups,
        shape((half, parent_links, rank * rank), BF16),
        [pltpu.VMEM((2, 4 * rank, 2 * rank), F32)],
        "parent_couple", 16, 4 * square * old, 4 * square,
    )(parent_partner_group, parent_partner_slot, parent_half, *parents_held)
    return (new_leaf_bases, new_leaf_blocks, new_parent_blocks)


def solution(mesh):
    first = ("grp", "sub")
    placed = (
        P(first, None, None),
        P(first, None, None),
        P(first, None, None, None),
        P(first, None),
        P(first, None),
        P(first, None, None, None),
        P(first, None),
        P(first, None),
        P(),
        P(),
    )
    return jax.shard_map(
        shards,
        mesh=mesh,
        in_specs=placed,
        out_specs=(P(first, None, None),) * 3,
        check_vma=False,
    )
```

```python
import functools

import jax
import jax.numpy as jnp
from jax import lax
from jax.experimental import pallas as pl
from jax.experimental.pallas import tpu as pltpu
from jax.sharding import PartitionSpec as P

F32 = jnp.float32
BF16 = jnp.bfloat16
PIVOTS = 8
PANEL = 16
MIB = 1 << 20


def cat(parts, axis):
    return jnp.concatenate(parts, axis=axis)


def halves(value):
    high = value.astype(BF16)
    low = (value - high.astype(F32)).astype(BF16)
    return high, low


def dot(left, right):
    return lax.dot_general(left, right, (((1,), (0,)), ((), ())), preferred_element_type=F32)


def dot_t(left, right):
    return lax.dot_general(left, right, (((1,), (1,)), ((), ())), preferred_element_type=F32)


def fold(value):
    width = value.shape[1] // 2
    return value[:, :width] + value[:, width:]


def wide(value):
    return cat(halves(value), 1)


def tall(value):
    both = wide(value)
    return cat([both, both], 0)


def gram_sum(parts):
    row = cat(parts, 1)
    return dot_t(row, row)


def thirds(value):
    high, rest = halves_left(value)
    middle, rest = halves_left(rest)
    return high, middle, rest.astype(BF16)


def halves_left(value):
    high = value.astype(BF16)
    return high, value - high.astype(F32)


def eliminate(grid, made, turned, rank, pairs):
    shape = (8, 128)
    lane = lax.broadcasted_iota(jnp.int32, shape, 1)
    half = jnp.where(lane < rank, 0, rank)
    local = lane - half

    def spread(value, column):
        return jnp.take_along_axis(value, half + column, axis=1)

    for top in range(0, rank, PANEL):
        end = top + PANEL
        panel = [grid[8 * i : 8 * i + 8, :] for i in range(top, end)]
        for first in range(top, end, PIVOTS):
            last = first + PIVOTS
            rows = panel[first - top : last - top]
            corner = [[None] * PIVOTS for _ in range(PIVOTS)]
            for p in range(PIVOTS):
                for q in range(p, PIVOTS):
                    corner[p][q] = spread(rows[p], first + q)
            inside = (local >= first) & (local < last)
            rows = [
                jnp.where(inside, (local == first + p).astype(F32), rows[p])
                for p in range(PIVOTS)
            ]
            inverse = []
            for p in range(PIVOTS):
                inverse.append(1.0 / corner[p][p])
                for q in range(p + 1, PIVOTS):
                    factor = corner[p][q] * inverse[p]
                    for s in range(q, PIVOTS):
                        corner[q][s] = corner[q][s] - factor * corner[p][s]
                    rows[q] = rows[q] - factor * rows[p]
            scaled = [rows[p] * inverse[p] for p in range(PIVOTS)]
            for i in range(last, end):
                row = jnp.where(inside, 0.0, panel[i - top])
                for p in range(PIVOTS):
                    row = row - spread(scaled[p], i) * rows[p]
                panel[i - top] = row
            for p in range(PIVOTS):
                i = first + p
                done = jnp.where(local < last, rows[p] * lax.rsqrt(corner[p][p]), 0.0)
                made[8 * i : 8 * i + 8, :] = done
                if end < rank:
                    kept = rows[p]
                    if last < end:
                        kept = jnp.where((local < last) | (local >= end), kept, 0.0)
                    grid[8 * i : 8 * i + 8, :] = kept
                    at = 8 * (i - top)
                    turned[at : at + 8, :] = scaled[p]
        if end < rank:
            lane_below = lax.broadcasted_iota(jnp.int32, (rank - end, 2 * rank), 1)
            low = lane_below < rank
            local_below = lane_below - jnp.where(low, 0, rank)
            past = (local_below >= top) & (local_below < end)
            for pair in range(pairs):
                a, b, c = thirds(turned[pl.ds(pair, PANEL, stride=8), :])
                x, y, z = thirds(grid[pl.ds(8 * top + pair, PANEL, stride=8), :])
                full = lax.dot_general(
                    cat([a, a, a, b, b, c], 0), cat([x, y, z, x, y, x], 0),
                    (((0,), (0,)), ((), ())), preferred_element_type=F32,
                )
                full = jnp.where(low, full[end:rank], full[rank + end :])
                spot = pl.ds(8 * end + pair, rank - end, stride=8)
                grid[spot, :] = jnp.where(past, 0.0, grid[spot, :]) - full


def pair_rows(made, stored, pair, rank):
    wide_rank = 2 * rank
    factor = wide(made[pl.ds(pair, rank, stride=8), :])
    both = stored[pair]
    zero = jnp.zeros((rank, both.shape[1]), F32)
    spread = cat([cat([both[:rank], zero], 1), cat([zero, both[rank:]], 1)], 0)
    high, low = halves(spread)
    return dot(factor, cat([high, high], 0)) + dot(factor, cat([low, low], 0))


def store_gram(grid, stored, pair, images, rank):
    both = cat(images, 0)
    stored[pair] = both
    both_wide = wide(both)
    high, low = halves(both)
    full = dot_t(both_wide, cat([cat([high, high], 1), cat([low, low], 1)], 0))
    full = fold(full)
    lane = lax.broadcasted_iota(jnp.int32, (rank, 2 * rank), 1)
    grid[pl.ds(pair, rank, stride=8), :] = jnp.where(lane < rank, full[:rank], full[rank:])


def sent_weights(blocks, weight):
    half = weight.shape[0]
    start = (1 - lax.axis_index("sub") % 2) * half
    for j in range(half):
        weight[j] = gram_sum([blocks[start + j, c] for c in range(blocks.shape[1])])


def kept_weights(blocks, parents, weight, parent_weight):
    half = weight.shape[0]
    start = (lax.axis_index("sub") % 2) * half
    for j in range(half):
        weight[j] = gram_sum([blocks[start + j, c] for c in range(blocks.shape[1])])
        parent_weight[j] = gram_sum([parents[j, c] for c in range(parents.shape[1])])


def images_of(starts, weights):
    folded = [tall(weight) for weight in weights]
    images = [fold(dot(starts, each)) for each in folded]
    return [fold(dot(wide(image), each)) for image, each in zip(images, folded)]


def leaf_step(own, other, parent, transfers, other_transfers, start, change, stacked, grid, made, turned, stored):
    rank = start.shape[0]
    half = own.shape[0]
    member = lax.axis_index("sub") % 2
    first = member * half
    moves = [(transfers[first + j], other_transfers[first + j]) for j in range(half)]
    size = parent.shape[1]
    carried = [fold(dot(cat(moves[j], 0), wide(parent[j]))) for j in range(half)]
    weights = []
    for j in range(half):
        for at, base in enumerate((own[j], other[j])):
            part = wide(carried[j][at * size : at * size + size])
            weights.append(base + dot_t(part, cat([moves[j][at]] * 2, 1)))
    images = images_of(wide(start[...]), weights)
    for j in range(half):
        store_gram(grid, stored, j, images[2 * j : 2 * j + 2], rank)
    eliminate(grid, made, turned, rank, half)
    found = [pair_rows(made, stored, j, rank).astype(BF16) for j in range(half)]
    for j in range(half):
        width = found[j].shape[1] // 2
        mine, theirs = found[j][:, :width], found[j][:, width:]
        change[0, j] = mine
        change[1, j] = theirs
        stacked[j, member] = dot(mine, moves[j][0])
        stacked[j, 1 - member] = dot(theirs, moves[j][1])


def parent_step(parent, stacked, start, change, grid, made, turned, stored):
    rank = start.shape[0]
    half = parent.shape[0]
    rows = [cat([stacked[j, 0], stacked[j, 1]], 0) for j in range(half)]
    left = [fold(dot(wide(rows[j]), tall(parent[j]))) for j in range(half)]
    grams = []
    for j in range(half):
        high, low = halves(rows[j])
        right = cat([cat([high, high], 1), cat([low, low], 1)], 0)
        grams.append(fold(dot_t(wide(left[j]), right)))
    images = images_of(wide(start[...]), grams)
    for pair in range(half // 2):
        store_gram(grid, stored, pair, images[2 * pair : 2 * pair + 2], rank)
    eliminate(grid, made, turned, rank, half // 2)
    found = [pair_rows(made, stored, pair, rank) for pair in range(half // 2)]
    for j in range(half):
        width = found[0].shape[1] // 2
        at = j % 2 * width
        mixed = wide(found[j // 2][:, at : at + width])
        rows = tall(cat([stacked[j, 0], stacked[j, 1]], 0))
        change[j] = fold(dot(mixed, rows)).astype(BF16)


def parted(value, scratch):
    scratch[...] = value.astype(F32)
    count = value.shape[0] // 2
    return cat(
        [scratch[pl.ds(0, count, stride=2), :], scratch[pl.ds(1, count, stride=2), :]], 0
    ).astype(BF16)


def middle_step(
    change, swapped, parent_change, bases, blocks, parents, _,
    new_bases, leaf_half, parent_half, token,
    order, order_parents,
):
    token[...] = jnp.zeros(token.shape, token.dtype)
    half, links = parents.shape[0], blocks.shape[1]
    member = lax.axis_index("sub") % 2
    for at in range(2 * half):
        j = at % half
        spot = (member if at < half else 1 - member) * half + j
        rows = change[0, j] if at < half else swapped[1, j]
        ordered = parted(rows, order.at[at % 4])
        new_bases[spot] = dot_t(rows, bases[spot]).astype(BF16)
        leaf_half[spot] = dot(ordered, cat([blocks[spot, c] for c in range(links)], 1)).astype(BF16)
    for j in range(half):
        ordered = parted(parent_change[j], order_parents.at[j % 2])
        parent_half[j] = dot(
            ordered, cat([parents[j, c] for c in range(parents.shape[1])], 1)
        ).astype(BF16)


def pack(*refs):
    *parts, out = refs
    count = parts[0].shape[0]
    for at, part in enumerate(parts):
        out[at * count : at * count + count] = part[...]


def pause(_, token):
    token[...] = jnp.zeros(token.shape, token.dtype)


def couple(middle, partner, lanes_low):
    full = dot_t(middle, cat([partner, partner], 0))
    count = full.shape[0] // 2
    return jnp.where(lanes_low, full[:count], full[count:])


def write_rows(out, at, order, links, count):
    for m in range(count):
        out[at, :, m * 128 : m * 128 + 128] = order[8 * m : 8 * m + links, :].astype(BF16)


def leaf_couple(boxes, devs_in, slots_in, middle, _, *rest):
    held_boxes, (out, token, devs, slots, held, order, sems) = rest[:-7], rest[-7:]
    token[...] = jnp.zeros(token.shape, token.dtype)
    count, links = out.shape[0], out.shape[1]
    half = count // 2
    rank = middle.shape[1]
    index = lax.axis_index("sub")
    member, chip = index % 2, index // 2
    copies = [
        pltpu.make_async_copy(devs_in, devs, sems.at[0]),
        pltpu.make_async_copy(slots_in, slots, sems.at[1]),
    ]
    for copy in copies:
        copy.start()
    for box, source in zip(boxes, held_boxes):
        for at, place in enumerate(box):
            held[place] = source[2 * at : 2 * at + 2]
    for copy in copies:
        copy.wait()
    low = lax.broadcasted_iota(jnp.int32, (rank // 2, 2 * rank), 1) < rank
    for t in range(count):
        for c in range(links):
            dev, slot = devs[c, t], slots[c, t]
            side = jnp.where(slot >= half, 1, 0)
            place = slot - side * half
            box = ((dev // 2) ^ chip) * 2 + (side ^ member)
            partner = held[box, (dev % 2) ^ side, place]
            order[t % 4, pl.ds(c, rank // 2, stride=8), :] = couple(
                middle[t, :, c * 128 : c * 128 + 128], partner, low
            )
        write_rows(out, t, order.at[t % 4], links, rank // 2)


def parent_couple(groups_in, slots_in, middle, _, *rest):
    boxes = len(rest) - 6
    near = rest[:boxes]
    out, groups, slots, held, order, sems = rest[boxes:]
    count, links = out.shape[0], out.shape[1]
    rank = middle.shape[1]
    mine = lax.axis_index("grp")
    copies = [
        pltpu.make_async_copy(groups_in, groups, sems.at[0]),
        pltpu.make_async_copy(slots_in, slots, sems.at[1]),
    ]
    for copy in copies:
        copy.start()
    for m in range(boxes):
        held[m] = near[m][...]
    for copy in copies:
        copy.wait()
    low = lax.broadcasted_iota(jnp.int32, (rank // 2, 2 * rank), 1) < rank
    for p in range(count):
        for c in range(links):
            partner = held[groups[c, p] ^ mine, slots[c, p]]
            order[p % 2, pl.ds(c, rank // 2, stride=8), :] = couple(
                middle[p, :, c * 128 : c * 128 + 128], partner, low
            )
        write_rows(out, p, order.at[p % 2], links, rank // 2)


VMEM = pl.BlockSpec(memory_space=pltpu.VMEM)
ANY = pl.BlockSpec(memory_space=pl.ANY)
HBM = pl.BlockSpec(memory_space=pltpu.HBM)


def call(body, ins, out_shapes, scratch, name, mib, flops, moved):
    many = isinstance(out_shapes, list)
    return pl.pallas_call(
        body,
        out_shape=out_shapes,
        in_specs=ins,
        out_specs=[VMEM] * len(out_shapes) if many else VMEM,
        scratch_shapes=scratch,
        name=name,
        compiler_params=pltpu.CompilerParams(vmem_limit_bytes=mib * MIB),
        cost_estimate=pl.CostEstimate(flops=flops, bytes_accessed=moved, transcendentals=0),
    )


def swap(block, axis, mask):
    count = lax.axis_size(axis)
    return lax.ppermute(block, axis, [(i, i ^ mask) for i in range(count)])


def shards(
    leaf_bases,
    leaf_transfers,
    leaf_blocks,
    leaf_partner_dev,
    leaf_partner_slot,
    parent_blocks,
    parent_partner_group,
    parent_partner_slot,
    leaf_start,
    parent_start,
):
    count, links, old = leaf_blocks.shape[:3]
    half, parent_links = parent_blocks.shape[:2]
    rank = leaf_start.shape[0]
    points = leaf_bases.shape[1]
    chips = lax.axis_size("sub") // 2
    groups = lax.axis_size("grp")
    shape = jax.ShapeDtypeStruct
    dma = pltpu.SemaphoreType.DMA
    square = half * old * old

    weights = shape((half, old, old), F32)
    other_transfers = swap(leaf_transfers, "sub", 1)
    sent = call(
        sent_weights, [VMEM], weights, [],
        "sent_weights", 8, 2 * links * square * old, 2 * links * square,
    )(leaf_blocks)
    other = swap(sent, "sub", 1)
    own, parent_weight = call(
        kept_weights, [VMEM] * 2, [weights, weights], [],
        "kept_weights", 8, 2 * (links + parent_links) * square * old, 8 * links * square,
    )(leaf_blocks, parent_blocks)
    tables = [
        pltpu.VMEM((8 * rank, 2 * rank), F32),
        pltpu.VMEM((8 * rank, 2 * rank), F32),
        pltpu.VMEM((8 * PANEL, 2 * rank), F32),
        pltpu.VMEM((half, 2 * rank, old), F32),
    ]
    change, stacked = call(
        leaf_step, [VMEM] * 6,
        [shape((2, half, rank, old), BF16), shape((half, 2, rank, old), F32)],
        tables, "leaf_step", 8, 40 * square * old, 8 * square,
    )(own, other, parent_weight, leaf_transfers, other_transfers, leaf_start)

    swapped = swap(change, "sub", 1)
    near = [swap(change, "sub", 2 * m) for m in range(1, chips)]
    parent_change = call(
        parent_step, [VMEM] * 3, shape((half, rank, old), BF16),
        tables, "parent_step", 8, 20 * square * old, 8 * square,
    )(parent_weight, stacked, parent_start)
    parents_held = [parent_change] + [
        swap(parent_change, "grp", m) for m in range(1, groups)
    ]
    token = shape((8, 128), F32)
    new_leaf_bases, leaf_half, parent_half, after_middle = call(
        middle_step, [VMEM] * 7,
        [
            shape((count, rank, points), BF16),
            shape((count, rank, links * old), BF16),
            shape((half, rank, parent_links * old), BF16),
            token,
        ],
        [pltpu.VMEM((4, rank, old), F32), pltpu.VMEM((2, rank, old), F32)],
        "middle_step", 8, 20 * square * old, 12 * links * square,
    )(change, swapped, parent_change, leaf_bases, leaf_blocks, parent_blocks, near[0])
    packed = call(
        pack, [VMEM] * (chips - 2), shape((2 * (chips - 2), half, rank, old), BF16), [],
        "pack", 2 + chips, square, square,
    )(*near[1:])
    paused = call(pause, [VMEM], token, [], "pause", 4, 1 << 34, square)(after_middle)
    held = [change, swapped, *near, swap(near[0], "sub", 1), swap(packed, "sub", 1)]
    boxes = [(0,), (1,)] + [(2 * m,) for m in range(1, chips)]
    boxes += [(3,), tuple(2 * m + 1 for m in range(2, chips))]
    table = pltpu.SMEM
    new_leaf_blocks, after_leaves = call(
        functools.partial(leaf_couple, boxes), [ANY, ANY] + [VMEM] * (2 + len(held)),
        [shape((count, links, rank * rank), BF16), token],
        [
            table((links, count), jnp.int32),
            table((links, count), jnp.int32),
            pltpu.VMEM((2 * chips, 2, half, rank, old), BF16),
            pltpu.VMEM((4, 4 * rank, 2 * rank), F32),
            dma((2,)),
        ],
        "leaf_couple", 4 + chips, 1 << 34, 12 * square,
    )(leaf_partner_dev.T, leaf_partner_slot.T, leaf_half, paused, *held)
    new_parent_blocks = call(
        parent_couple, [ANY, ANY] + [VMEM] * (groups + 2),
        shape((half, parent_links, rank * rank), BF16),
        [
            table((parent_links, half), jnp.int32),
            table((parent_links, half), jnp.int32),
            pltpu.VMEM((groups, half, rank, old), BF16),
            pltpu.VMEM((2, 4 * rank, 2 * rank), F32),
            dma((2,)),
        ],
        "parent_couple", 4 + groups, square, 4 * square,
    )(parent_partner_group.T, parent_partner_slot.T, parent_half, after_leaves, *parents_held)
    return (new_leaf_bases, new_leaf_blocks, new_parent_blocks)


def solution(mesh):
    first = ("grp", "sub")
    placed = (
        P(first, None, None),
        P(first, None, None),
        P(first, None, None, None),
        P(first, None),
        P(first, None),
        P(first, None, None, None),
        P(first, None),
        P(first, None),
        P(),
        P(),
    )
    return jax.shard_map(
        shards,
        mesh=mesh,
        in_specs=placed,
        out_specs=(P(first, None, None),) * 3,
        check_vma=False,
    )
```

```python
import functools

import jax
import jax.numpy as jnp
from jax import lax
from jax.experimental import pallas as pl
from jax.experimental.pallas import tpu as pltpu
from jax.sharding import PartitionSpec as P

F32 = jnp.float32
BF16 = jnp.bfloat16
PIVOTS = 8
PANEL = 16
MIB = 1 << 20


def cat(parts, axis):
    return jnp.concatenate(parts, axis=axis)


def halves(value):
    high = value.astype(BF16)
    low = (value - high.astype(F32)).astype(BF16)
    return high, low


def dot(left, right):
    return lax.dot_general(left, right, (((1,), (0,)), ((), ())), preferred_element_type=F32)


def dot_t(left, right):
    return lax.dot_general(left, right, (((1,), (1,)), ((), ())), preferred_element_type=F32)


def fold(value):
    width = value.shape[1] // 2
    return value[:, :width] + value[:, width:]


def wide(value):
    return cat(halves(value), 1)


def tall(value):
    both = wide(value)
    return cat([both, both], 0)


def gram_sum(parts):
    row = cat(parts, 1)
    return dot_t(row, row)


def thirds(value):
    high, rest = halves_left(value)
    middle, rest = halves_left(rest)
    return high, middle, rest.astype(BF16)


def halves_left(value):
    high = value.astype(BF16)
    return high, value - high.astype(F32)


def eliminate(grid, made, turned, rank, pairs):
    shape = (8, 128)
    lane = lax.broadcasted_iota(jnp.int32, shape, 1)
    half = jnp.where(lane < rank, 0, rank)
    local = lane - half

    def spread(value, column):
        return jnp.take_along_axis(value, half + column, axis=1)

    for top in range(0, rank, PANEL):
        end = top + PANEL
        panel = [grid[8 * i : 8 * i + 8, :] for i in range(top, end)]
        for first in range(top, end, PIVOTS):
            last = first + PIVOTS
            rows = panel[first - top : last - top]
            corner = [[None] * PIVOTS for _ in range(PIVOTS)]
            for p in range(PIVOTS):
                for q in range(p, PIVOTS):
                    corner[p][q] = spread(rows[p], first + q)
            inside = (local >= first) & (local < last)
            rows = [
                jnp.where(inside, (local == first + p).astype(F32), rows[p])
                for p in range(PIVOTS)
            ]
            inverse = []
            for p in range(PIVOTS):
                inverse.append(1.0 / corner[p][p])
                for q in range(p + 1, PIVOTS):
                    factor = corner[p][q] * inverse[p]
                    for s in range(q, PIVOTS):
                        corner[q][s] = corner[q][s] - factor * corner[p][s]
                    rows[q] = rows[q] - factor * rows[p]
            scaled = [rows[p] * inverse[p] for p in range(PIVOTS)]
            for i in range(last, end):
                row = jnp.where(inside, 0.0, panel[i - top])
                for p in range(PIVOTS):
                    row = row - spread(scaled[p], i) * rows[p]
                panel[i - top] = row
            for p in range(PIVOTS):
                i = first + p
                done = jnp.where(local < last, rows[p] * lax.rsqrt(corner[p][p]), 0.0)
                made[8 * i : 8 * i + 8, :] = done
                if end < rank:
                    kept = rows[p]
                    if last < end:
                        kept = jnp.where((local < last) | (local >= end), kept, 0.0)
                    grid[8 * i : 8 * i + 8, :] = kept
                    at = 8 * (i - top)
                    turned[at : at + 8, :] = scaled[p]
        if end < rank:
            lane_below = lax.broadcasted_iota(jnp.int32, (rank - end, 2 * rank), 1)
            low = lane_below < rank
            local_below = lane_below - jnp.where(low, 0, rank)
            past = (local_below >= top) & (local_below < end)
            for pair in range(pairs):
                a, b, c = thirds(turned[pl.ds(pair, PANEL, stride=8), :])
                x, y, z = thirds(grid[pl.ds(8 * top + pair, PANEL, stride=8), :])
                full = lax.dot_general(
                    cat([a, a, a, b, b, c], 0), cat([x, y, z, x, y, x], 0),
                    (((0,), (0,)), ((), ())), preferred_element_type=F32,
                )
                full = jnp.where(low, full[end:rank], full[rank + end :])
                spot = pl.ds(8 * end + pair, rank - end, stride=8)
                grid[spot, :] = jnp.where(past, 0.0, grid[spot, :]) - full


def pair_rows(made, stored, pair, rank):
    wide_rank = 2 * rank
    factor = wide(made[pl.ds(pair, rank, stride=8), :])
    both = stored[pair]
    zero = jnp.zeros((rank, both.shape[1]), F32)
    spread = cat([cat([both[:rank], zero], 1), cat([zero, both[rank:]], 1)], 0)
    high, low = halves(spread)
    return dot(factor, cat([high, high], 0)) + dot(factor, cat([low, low], 0))


def store_gram(grid, stored, pair, images, rank):
    both = cat(images, 0)
    stored[pair] = both
    both_wide = wide(both)
    high, low = halves(both)
    full = dot_t(both_wide, cat([cat([high, high], 1), cat([low, low], 1)], 0))
    full = fold(full)
    lane = lax.broadcasted_iota(jnp.int32, (rank, 2 * rank), 1)
    grid[pl.ds(pair, rank, stride=8), :] = jnp.where(lane < rank, full[:rank], full[rank:])


def sent_weights(blocks, weight):
    half = weight.shape[0]
    start = (1 - lax.axis_index("sub") % 2) * half
    for j in range(half):
        weight[j] = gram_sum([blocks[start + j, c] for c in range(blocks.shape[1])])


def kept_weights(
    blocks, parents, devs, slots, groups, parent_slots,
    weight, parent_weight, leaf_table, parent_table,
):
    half = weight.shape[0]
    index = lax.axis_index("sub")
    member, chip = index & 1, index >> 1
    dev, slot = devs[...], slots[...]
    side = jnp.where(slot >= half, 1, 0)
    box = ((dev >> 1) ^ chip) * 2 + (side ^ member)
    leaf_table[...] = (box * 2 + ((dev & 1) ^ side)) * half + slot - side * half
    parent_table[...] = (groups[...] ^ lax.axis_index("grp")) * half + parent_slots[...]
    start = (lax.axis_index("sub") % 2) * half
    for j in range(half):
        weight[j] = gram_sum([blocks[start + j, c] for c in range(blocks.shape[1])])
        parent_weight[j] = gram_sum([parents[j, c] for c in range(parents.shape[1])])


def images_of(starts, weights):
    folded = [tall(weight) for weight in weights]
    images = [fold(dot(starts, each)) for each in folded]
    return [fold(dot(wide(image), each)) for image, each in zip(images, folded)]


def leaf_step(own, other, parent, transfers, other_transfers, start, change, stacked, grid, made, turned, stored):
    rank = start.shape[0]
    half = own.shape[0]
    member = lax.axis_index("sub") % 2
    first = member * half
    moves = [(transfers[first + j], other_transfers[first + j]) for j in range(half)]
    size = parent.shape[1]
    carried = [fold(dot(cat(moves[j], 0), wide(parent[j]))) for j in range(half)]
    weights = []
    for j in range(half):
        for at, base in enumerate((own[j], other[j])):
            part = wide(carried[j][at * size : at * size + size])
            weights.append(base + dot_t(part, cat([moves[j][at]] * 2, 1)))
    images = images_of(wide(start[...]), weights)
    for j in range(half):
        store_gram(grid, stored, j, images[2 * j : 2 * j + 2], rank)
    eliminate(grid, made, turned, rank, half)
    found = [pair_rows(made, stored, j, rank).astype(BF16) for j in range(half)]
    for j in range(half):
        width = found[j].shape[1] // 2
        mine, theirs = found[j][:, :width], found[j][:, width:]
        change[0, j] = mine
        change[1, j] = theirs
        stacked[j, member] = dot(mine, moves[j][0])
        stacked[j, 1 - member] = dot(theirs, moves[j][1])


def parent_step(parent, stacked, start, change, grid, made, turned, stored):
    rank = start.shape[0]
    half = parent.shape[0]
    rows = [cat([stacked[j, 0], stacked[j, 1]], 0) for j in range(half)]
    left = [fold(dot(wide(rows[j]), tall(parent[j]))) for j in range(half)]
    grams = []
    for j in range(half):
        high, low = halves(rows[j])
        right = cat([cat([high, high], 1), cat([low, low], 1)], 0)
        grams.append(fold(dot_t(wide(left[j]), right)))
    images = images_of(wide(start[...]), grams)
    for pair in range(half // 2):
        store_gram(grid, stored, pair, images[2 * pair : 2 * pair + 2], rank)
    eliminate(grid, made, turned, rank, half // 2)
    found = [pair_rows(made, stored, pair, rank) for pair in range(half // 2)]
    for j in range(half):
        width = found[0].shape[1] // 2
        at = j % 2 * width
        mixed = wide(found[j // 2][:, at : at + width])
        rows = tall(cat([stacked[j, 0], stacked[j, 1]], 0))
        change[j] = fold(dot(mixed, rows)).astype(BF16)


def parted(value, scratch):
    scratch[...] = value.astype(F32)
    count = value.shape[0] // 2
    return cat(
        [scratch[pl.ds(0, count, stride=2), :], scratch[pl.ds(1, count, stride=2), :]], 0
    ).astype(BF16)


def middle_own(
    change, parent_change, bases, blocks, parents, _,
    own_bases, own_half, parent_half, token,
    order, order_parents,
):
    token[...] = jnp.zeros(token.shape, token.dtype)
    half, links = parents.shape[0], blocks.shape[1]
    first = (lax.axis_index("sub") % 2) * half
    for j in range(half):
        rows = change[0, j]
        ordered = parted(rows, order.at[j % 4])
        own_bases[j] = dot_t(rows, bases[first + j]).astype(BF16)
        own_half[j] = dot(ordered, cat([blocks[first + j, c] for c in range(links)], 1)).astype(BF16)
    for j in range(half):
        ordered = parted(parent_change[j], order_parents.at[j % 4])
        parent_half[j] = dot(
            ordered, cat([parents[j, c] for c in range(parents.shape[1])], 1)
        ).astype(BF16)


def middle_other(swapped, bases, blocks, own_bases, _, new_bases, other_half, order):
    half, links = own_bases.shape[0], blocks.shape[1]
    member = lax.axis_index("sub") % 2
    first = (1 - member) * half
    new_bases[pl.ds(member * half, half)] = own_bases[...]
    for j in range(half):
        rows = swapped[1, j]
        ordered = parted(rows, order.at[j % 4])
        new_bases[first + j] = dot_t(rows, bases[first + j]).astype(BF16)
        other_half[j] = dot(
            ordered, cat([blocks[first + j, c] for c in range(links)], 1)
        ).astype(BF16)


def pack(*refs):
    _, *parts, out = refs
    count = parts[0].shape[0]
    for at, part in enumerate(parts):
        out[at * count : at * count + count] = part[...]


def pause(_, token):
    token[...] = jnp.zeros(token.shape, token.dtype)


def couple(middle, partner):
    full = dot_t(middle, partner)
    count = full.shape[0] // 2
    return cat([full[:count], full[count:]], 1)


def write_rows(out, at, order, links, count):
    for m in range(count):
        out[at, :, m * 128 : m * 128 + 128] = order[8 * m : 8 * m + links, :].astype(BF16)


def leaf_couple(boxes, table_in, own_half, other_half, _, *rest):
    held_boxes, (out, token, table, held, order, sem) = rest[:-6], rest[-6:]
    count, links = out.shape[0], out.shape[1]
    half, rank = own_half.shape[:2]
    member = lax.axis_index("sub") % 2
    copy = pltpu.make_async_copy(table_in, table, sem)
    copy.start()
    token[...] = jnp.zeros(token.shape, token.dtype)
    size = 2 * held_boxes[0].shape[1]
    for box, source in zip(boxes, held_boxes):
        for at, place in enumerate(box):
            part = source[2 * at : 2 * at + 2]
            held[place * size : place * size + size] = part.reshape((size,) + part.shape[2:])
    copy.wait()
    for at in range(count):
        own = at < half
        middle = own_half if own else other_half
        j = at % half
        t = (member if own else 1 - member) * half + j
        for c in range(links):
            order[at % 4, pl.ds(c, rank // 2, stride=8), :] = couple(
                middle[j, :, c * 128 : c * 128 + 128], held[table[c, t]]
            )
        write_rows(out, t, order.at[at % 4], links, rank // 2)


def parent_couple(table_in, middle, _, *rest):
    near, (out, table, held, order, sem) = rest[:-5], rest[-5:]
    count, links = out.shape[0], out.shape[1]
    rank = middle.shape[1]
    copy = pltpu.make_async_copy(table_in, table, sem)
    copy.start()
    for m in range(len(near)):
        held[m * count : m * count + count] = near[m][...]
    copy.wait()
    for p in range(count):
        for c in range(links):
            order[p % 2, pl.ds(c, rank // 2, stride=8), :] = couple(
                middle[p, :, c * 128 : c * 128 + 128], held[table[c, p]]
            )
        write_rows(out, p, order.at[p % 2], links, rank // 2)


VMEM = pl.BlockSpec(memory_space=pltpu.VMEM)
ANY = pl.BlockSpec(memory_space=pl.ANY)
HBM = pl.BlockSpec(memory_space=pltpu.HBM)


def call(body, ins, out_shapes, scratch, name, mib, flops, moved):
    many = isinstance(out_shapes, list)
    return pl.pallas_call(
        body,
        out_shape=out_shapes,
        in_specs=ins,
        out_specs=[VMEM] * len(out_shapes) if many else VMEM,
        scratch_shapes=scratch,
        name=name,
        compiler_params=pltpu.CompilerParams(vmem_limit_bytes=mib * MIB),
        cost_estimate=pl.CostEstimate(flops=flops, bytes_accessed=moved, transcendentals=0),
    )


def swap(block, axis, mask):
    count = lax.axis_size(axis)
    return lax.ppermute(block, axis, [(i, i ^ mask) for i in range(count)])


def shards(
    leaf_bases,
    leaf_transfers,
    leaf_blocks,
    leaf_partner_dev,
    leaf_partner_slot,
    parent_blocks,
    parent_partner_group,
    parent_partner_slot,
    leaf_start,
    parent_start,
):
    count, links, old = leaf_blocks.shape[:3]
    half, parent_links = parent_blocks.shape[:2]
    rank = leaf_start.shape[0]
    points = leaf_bases.shape[1]
    chips = lax.axis_size("sub") // 2
    groups = lax.axis_size("grp")
    shape = jax.ShapeDtypeStruct
    dma = pltpu.SemaphoreType.DMA
    square = half * old * old

    weights = shape((half, old, old), F32)
    other_transfers = swap(leaf_transfers, "sub", 1)
    sent = call(
        sent_weights, [VMEM], weights, [],
        "sent_weights", 8, 2 * links * square * old, 2 * links * square,
    )(leaf_blocks)
    other = swap(sent, "sub", 1)
    own, parent_weight, leaf_table, parent_table = call(
        kept_weights, [VMEM] * 6,
        [weights, weights, shape((links, count), jnp.int32), shape((parent_links, half), jnp.int32)],
        [],
        "kept_weights", 8, 2 * (links + parent_links) * square * old, 8 * links * square,
    )(
        leaf_blocks, parent_blocks,
        leaf_partner_dev.T, leaf_partner_slot.T, parent_partner_group.T, parent_partner_slot.T,
    )
    tables = [
        pltpu.VMEM((8 * rank, 2 * rank), F32),
        pltpu.VMEM((8 * rank, 2 * rank), F32),
        pltpu.VMEM((8 * PANEL, 2 * rank), F32),
        pltpu.VMEM((half, 2 * rank, old), F32),
    ]
    change, stacked = call(
        leaf_step, [VMEM] * 6,
        [shape((2, half, rank, old), BF16), shape((half, 2, rank, old), F32)],
        tables, "leaf_step", 8, 40 * square * old, 8 * square,
    )(own, other, parent_weight, leaf_transfers, other_transfers, leaf_start)

    swapped = swap(change, "sub", 1)
    near = [swap(change, "sub", 2 * m) for m in range(1, chips)]
    parent_change = call(
        parent_step, [VMEM] * 3, shape((half, rank, old), BF16),
        tables, "parent_step", 8, 20 * square * old, 8 * square,
    )(parent_weight, stacked, parent_start)
    parents_held = [parent_change] + [
        swap(parent_change, "grp", m) for m in range(1, groups)
    ]
    token = shape((8, 128), F32)
    half_shape = shape((half, rank, links * old), BF16)
    own_bases, own_half, parent_half, after_middle = call(
        middle_own, [VMEM] * 6,
        [
            shape((half, rank, points), BF16), half_shape,
            shape((half, rank, parent_links * old), BF16), token,
        ],
        [pltpu.VMEM((4, rank, old), F32), pltpu.VMEM((4, rank, old), F32)],
        "middle_own", 8, 1 << 34, square,
    )(change, parent_change, leaf_bases, leaf_blocks, parent_blocks, swapped)
    packed = call(
        pack, [VMEM] * chips, shape((2 * chips - 2, half, rank, old), BF16), [],
        "pack", 4 + chips, 1 << 34, square,
    )(after_middle, *near)
    new_leaf_bases, other_half = call(
        middle_other, [VMEM] * 5, [shape((count, rank, points), BF16), half_shape],
        [pltpu.VMEM((4, rank, old), F32)],
        "middle_other", 8, square, square,
    )(swapped, leaf_bases, leaf_blocks, own_bases, packed)
    paused = call(pause, [VMEM], token, [], "pause", 4, 1 << 34, square)(packed)
    held = [change, swapped, *near, swap(packed, "sub", 1)]
    boxes = [(0,), (1,)] + [(2 * m,) for m in range(1, chips)]
    boxes += [tuple(2 * m + 1 for m in range(1, chips))]
    new_leaf_blocks, after_leaves = call(
        functools.partial(leaf_couple, boxes), [ANY] + [VMEM] * (3 + len(held)),
        [shape((count, links, rank * rank), BF16), token],
        [
            pltpu.SMEM((links, count), jnp.int32),
            pltpu.VMEM((2 * chips * count, rank, old), BF16),
            pltpu.VMEM((4, 4 * rank, 2 * rank), F32),
            dma(()),
        ],
        "leaf_couple", 4 + chips, 1 << 34, 12 * square,
    )(leaf_table, own_half, other_half, paused, *held)
    new_parent_blocks = call(
        parent_couple, [ANY] + [VMEM] * (groups + 2),
        shape((half, parent_links, rank * rank), BF16),
        [
            pltpu.SMEM((parent_links, half), jnp.int32),
            pltpu.VMEM((groups * half, rank, old), BF16),
            pltpu.VMEM((2, 4 * rank, 2 * rank), F32),
            dma(()),
        ],
        "parent_couple", 4 + groups, square, 4 * square,
    )(parent_table, parent_half, after_leaves, *parents_held)
    return (new_leaf_bases, new_leaf_blocks, new_parent_blocks)


def solution(mesh):
    first = ("grp", "sub")
    placed = (
        P(first, None, None),
        P(first, None, None),
        P(first, None, None, None),
        P(first, None),
        P(first, None),
        P(first, None, None, None),
        P(first, None),
        P(first, None),
        P(),
        P(),
    )
    return jax.shard_map(
        shards,
        mesh=mesh,
        in_specs=placed,
        out_specs=(P(first, None, None),) * 3,
        check_vma=False,
    )
```

```python
import functools

import jax
import jax.numpy as jnp
from jax import lax
from jax.experimental import pallas as pl
from jax.experimental.pallas import tpu as pltpu
from jax.sharding import PartitionSpec as P

F32 = jnp.float32
BF16 = jnp.bfloat16
PIVOTS = 8
PANEL = 16
MIB = 1 << 20


def cat(parts, axis):
    return jnp.concatenate(parts, axis=axis)


def halves(value):
    high = value.astype(BF16)
    low = (value - high.astype(F32)).astype(BF16)
    return high, low


def dot(left, right):
    return lax.dot_general(left, right, (((1,), (0,)), ((), ())), preferred_element_type=F32)


def dot_t(left, right):
    return lax.dot_general(left, right, (((1,), (1,)), ((), ())), preferred_element_type=F32)


def fold(value):
    width = value.shape[1] // 2
    return value[:, :width] + value[:, width:]


def wide(value):
    return cat(halves(value), 1)


def tall(value):
    both = wide(value)
    return cat([both, both], 0)


def gram_sum(parts):
    row = cat(parts, 1)
    return dot_t(row, row)


def thirds(value):
    high, rest = halves_left(value)
    middle, rest = halves_left(rest)
    return high, middle, rest.astype(BF16)


def halves_left(value):
    high = value.astype(BF16)
    return high, value - high.astype(F32)


def eliminate(grid, made, turned, rank, pairs):
    shape = (8, 128)
    lane = lax.broadcasted_iota(jnp.int32, shape, 1)
    half = jnp.where(lane < rank, 0, rank)
    local = lane - half

    def spread(value, column):
        return jnp.take_along_axis(value, half + column, axis=1)

    for top in range(0, rank, PANEL):
        end = top + PANEL
        panel = [grid[8 * i : 8 * i + 8, :] for i in range(top, end)]
        for first in range(top, end, PIVOTS):
            last = first + PIVOTS
            rows = panel[first - top : last - top]
            corner = [[None] * PIVOTS for _ in range(PIVOTS)]
            for p in range(PIVOTS):
                for q in range(p, PIVOTS):
                    corner[p][q] = spread(rows[p], first + q)
            inside = (local >= first) & (local < last)
            rows = [
                jnp.where(inside, (local == first + p).astype(F32), rows[p])
                for p in range(PIVOTS)
            ]
            inverse = []
            for p in range(PIVOTS):
                inverse.append(1.0 / corner[p][p])
                for q in range(p + 1, PIVOTS):
                    factor = corner[p][q] * inverse[p]
                    for s in range(q, PIVOTS):
                        corner[q][s] = corner[q][s] - factor * corner[p][s]
                    rows[q] = rows[q] - factor * rows[p]
            scaled = [rows[p] * inverse[p] for p in range(PIVOTS)]
            for i in range(last, end):
                row = jnp.where(inside, 0.0, panel[i - top])
                for p in range(PIVOTS):
                    row = row - spread(scaled[p], i) * rows[p]
                panel[i - top] = row
            for p in range(PIVOTS):
                i = first + p
                done = jnp.where(local < last, rows[p] * lax.rsqrt(corner[p][p]), 0.0)
                made[8 * i : 8 * i + 8, :] = done
                if end < rank:
                    kept = rows[p]
                    if last < end:
                        kept = jnp.where((local < last) | (local >= end), kept, 0.0)
                    grid[8 * i : 8 * i + 8, :] = kept
                    at = 8 * (i - top)
                    turned[at : at + 8, :] = scaled[p]
        if end < rank:
            lane_below = lax.broadcasted_iota(jnp.int32, (rank - end, 2 * rank), 1)
            low = lane_below < rank
            local_below = lane_below - jnp.where(low, 0, rank)
            past = (local_below >= top) & (local_below < end)
            for pair in range(pairs):
                a, b, c = thirds(turned[pl.ds(pair, PANEL, stride=8), :])
                x, y, z = thirds(grid[pl.ds(8 * top + pair, PANEL, stride=8), :])
                full = lax.dot_general(
                    cat([a, a, a, b, b, c], 0), cat([x, y, z, x, y, x], 0),
                    (((0,), (0,)), ((), ())), preferred_element_type=F32,
                )
                full = jnp.where(low, full[end:rank], full[rank + end :])
                spot = pl.ds(8 * end + pair, rank - end, stride=8)
                grid[spot, :] = jnp.where(past, 0.0, grid[spot, :]) - full


def pair_rows(made, stored, pair, rank):
    wide_rank = 2 * rank
    factor = wide(made[pl.ds(pair, rank, stride=8), :])
    both = stored[pair]
    zero = jnp.zeros((rank, both.shape[1]), F32)
    spread = cat([cat([both[:rank], zero], 1), cat([zero, both[rank:]], 1)], 0)
    high, low = halves(spread)
    return dot(factor, cat([high, high], 0)) + dot(factor, cat([low, low], 0))


def store_gram(grid, stored, pair, images, rank):
    both = cat(images, 0)
    stored[pair] = both
    both_wide = wide(both)
    high, low = halves(both)
    full = dot_t(both_wide, cat([cat([high, high], 1), cat([low, low], 1)], 0))
    full = fold(full)
    lane = lax.broadcasted_iota(jnp.int32, (rank, 2 * rank), 1)
    grid[pl.ds(pair, rank, stride=8), :] = jnp.where(lane < rank, full[:rank], full[rank:])


def sent_weights(blocks, weight):
    half = weight.shape[0]
    start = (1 - lax.axis_index("sub") % 2) * half
    for j in range(half):
        weight[j] = gram_sum([blocks[start + j, c] for c in range(blocks.shape[1])])


def kept_weights(
    blocks, parents, devs, slots, groups, parent_slots,
    weight, parent_weight, leaf_table, parent_table,
):
    half = weight.shape[0]
    index = lax.axis_index("sub")
    member, chip = index & 1, index >> 1
    dev, slot = devs[...], slots[...]
    side = jnp.where(slot >= half, 1, 0)
    box = ((dev >> 1) ^ chip) * 2 + (side ^ member)
    leaf_table[...] = (box * 2 + ((dev & 1) ^ side)) * half + slot - side * half
    parent_table[...] = (groups[...] ^ lax.axis_index("grp")) * half + parent_slots[...]
    start = (lax.axis_index("sub") % 2) * half
    for j in range(half):
        weight[j] = gram_sum([blocks[start + j, c] for c in range(blocks.shape[1])])
        parent_weight[j] = gram_sum([parents[j, c] for c in range(parents.shape[1])])


def images_of(starts, weights):
    folded = [tall(weight) for weight in weights]
    images = [fold(dot(starts, each)) for each in folded]
    return [fold(dot(wide(image), each)) for image, each in zip(images, folded)]


def leaf_step(own, other, parent, transfers, other_transfers, start, change, stacked, grid, made, turned, stored):
    rank = start.shape[0]
    half = own.shape[0]
    member = lax.axis_index("sub") % 2
    first = member * half
    moves = [(transfers[first + j], other_transfers[first + j]) for j in range(half)]
    size = parent.shape[1]
    carried = [fold(dot(cat(moves[j], 0), wide(parent[j]))) for j in range(half)]
    weights = []
    for j in range(half):
        for at, base in enumerate((own[j], other[j])):
            part = wide(carried[j][at * size : at * size + size])
            weights.append(base + dot_t(part, cat([moves[j][at]] * 2, 1)))
    images = images_of(wide(start[...]), weights)
    for j in range(half):
        store_gram(grid, stored, j, images[2 * j : 2 * j + 2], rank)
    eliminate(grid, made, turned, rank, half)
    found = [pair_rows(made, stored, j, rank).astype(BF16) for j in range(half)]
    for j in range(half):
        width = found[j].shape[1] // 2
        mine, theirs = found[j][:, :width], found[j][:, width:]
        change[0, j] = mine
        change[1, j] = theirs
        stacked[j, member] = dot(mine, moves[j][0])
        stacked[j, 1 - member] = dot(theirs, moves[j][1])


def parent_step(parent, stacked, start, change, grid, made, turned, stored):
    rank = start.shape[0]
    half = parent.shape[0]
    rows = [cat([stacked[j, 0], stacked[j, 1]], 0) for j in range(half)]
    left = [fold(dot(wide(rows[j]), tall(parent[j]))) for j in range(half)]
    grams = []
    for j in range(half):
        high, low = halves(rows[j])
        right = cat([cat([high, high], 1), cat([low, low], 1)], 0)
        grams.append(fold(dot_t(wide(left[j]), right)))
    images = images_of(wide(start[...]), grams)
    for pair in range(half // 2):
        store_gram(grid, stored, pair, images[2 * pair : 2 * pair + 2], rank)
    eliminate(grid, made, turned, rank, half // 2)
    found = [pair_rows(made, stored, pair, rank) for pair in range(half // 2)]
    for j in range(half):
        width = found[0].shape[1] // 2
        at = j % 2 * width
        mixed = wide(found[j // 2][:, at : at + width])
        rows = tall(cat([stacked[j, 0], stacked[j, 1]], 0))
        change[j] = fold(dot(mixed, rows)).astype(BF16)


def parted(value, scratch):
    scratch[...] = value.astype(F32)
    count = value.shape[0] // 2
    return cat(
        [scratch[pl.ds(0, count, stride=2), :], scratch[pl.ds(1, count, stride=2), :]], 0
    ).astype(BF16)


def middle_own(
    change, parent_change, bases, blocks, parents, _,
    own_bases, own_half, parent_half, token,
    order, order_parents,
):
    token[...] = jnp.zeros(token.shape, token.dtype)
    half, links = parents.shape[0], blocks.shape[1]
    first = (lax.axis_index("sub") % 2) * half
    for j in range(half):
        rows = change[0, j]
        ordered = parted(rows, order.at[j % 4])
        own_bases[j] = dot_t(rows, bases[first + j]).astype(BF16)
        own_half[j] = dot(ordered, cat([blocks[first + j, c] for c in range(links)], 1)).astype(BF16)
    for j in range(half):
        ordered = parted(parent_change[j], order_parents.at[j % 4])
        parent_half[j] = dot(
            ordered, cat([parents[j, c] for c in range(parents.shape[1])], 1)
        ).astype(BF16)


def middle_other(swapped, bases, blocks, own_bases, _, new_bases, other_half, order):
    half, links = own_bases.shape[0], blocks.shape[1]
    member = lax.axis_index("sub") % 2
    first = (1 - member) * half
    new_bases[pl.ds(member * half, half)] = own_bases[...]
    for j in range(half):
        rows = swapped[1, j]
        ordered = parted(rows, order.at[j % 4])
        new_bases[first + j] = dot_t(rows, bases[first + j]).astype(BF16)
        other_half[j] = dot(
            ordered, cat([blocks[first + j, c] for c in range(links)], 1)
        ).astype(BF16)


def pack(*refs):
    _, *parts, out = refs
    count = parts[0].shape[0]
    for at, part in enumerate(parts):
        out[at * count : at * count + count] = part[...]


def pause(_, token):
    token[...] = jnp.zeros(token.shape, token.dtype)


def couple(middle, partner):
    full = dot_t(middle, partner)
    count = full.shape[0] // 2
    return cat([full[:count], full[count:]], 1)


def write_rows(out, at, order, links, count):
    for m in range(count):
        out[at, :, m * 128 : m * 128 + 128] = order[8 * m : 8 * m + links, :].astype(BF16)


def leaf_couple(boxes, table_in, own_half, other_half, _, *rest):
    held_boxes, (out, token, held, order) = rest[:-4], rest[-4:]
    table = table_in[...]
    count, links = out.shape[0], out.shape[1]
    half, rank = own_half.shape[:2]
    member = lax.axis_index("sub") % 2
    token[...] = jnp.zeros(token.shape, token.dtype)
    size = 2 * held_boxes[0].shape[1]
    for box, source in zip(boxes, held_boxes):
        for at, place in enumerate(box):
            part = source[2 * at : 2 * at + 2]
            held[place * size : place * size + size] = part.reshape((size,) + part.shape[2:])
    for at in range(count):
        own = at < half
        middle = own_half if own else other_half
        j = at % half
        t = (member if own else 1 - member) * half + j
        rows = jnp.where(member == (0 if own else 1), table[:, j : j + 1], table[:, half + j : half + j + 1])
        for c in range(links):
            order[at % 4, pl.ds(c, rank // 2, stride=8), :] = couple(
                middle[j, :, c * 128 : c * 128 + 128], held[rows[c, 0]]
            )
        write_rows(out, t, order.at[at % 4], links, rank // 2)


def parent_couple(table_in, middle, _, *rest):
    near, (out, held, order) = rest[:-3], rest[-3:]
    table = table_in[...]
    count, links = out.shape[0], out.shape[1]
    rank = middle.shape[1]
    for m in range(len(near)):
        held[m * count : m * count + count] = near[m][...]
    for p in range(count):
        for c in range(links):
            order[p % 2, pl.ds(c, rank // 2, stride=8), :] = couple(
                middle[p, :, c * 128 : c * 128 + 128], held[table[c, p]]
            )
        write_rows(out, p, order.at[p % 2], links, rank // 2)


VMEM = pl.BlockSpec(memory_space=pltpu.VMEM)
ANY = pl.BlockSpec(memory_space=pl.ANY)
HBM = pl.BlockSpec(memory_space=pltpu.HBM)


def call(body, ins, out_shapes, scratch, name, mib, flops, moved):
    many = isinstance(out_shapes, list)
    return pl.pallas_call(
        body,
        out_shape=out_shapes,
        in_specs=ins,
        out_specs=[VMEM] * len(out_shapes) if many else VMEM,
        scratch_shapes=scratch,
        name=name,
        compiler_params=pltpu.CompilerParams(vmem_limit_bytes=mib * MIB),
        cost_estimate=pl.CostEstimate(flops=flops, bytes_accessed=moved, transcendentals=0),
    )


def swap(block, axis, mask):
    count = lax.axis_size(axis)
    return lax.ppermute(block, axis, [(i, i ^ mask) for i in range(count)])


def shards(
    leaf_bases,
    leaf_transfers,
    leaf_blocks,
    leaf_partner_dev,
    leaf_partner_slot,
    parent_blocks,
    parent_partner_group,
    parent_partner_slot,
    leaf_start,
    parent_start,
):
    count, links, old = leaf_blocks.shape[:3]
    half, parent_links = parent_blocks.shape[:2]
    rank = leaf_start.shape[0]
    points = leaf_bases.shape[1]
    chips = lax.axis_size("sub") // 2
    groups = lax.axis_size("grp")
    shape = jax.ShapeDtypeStruct
    dma = pltpu.SemaphoreType.DMA
    square = half * old * old

    weights = shape((half, old, old), F32)
    other_transfers = swap(leaf_transfers, "sub", 1)
    sent = call(
        sent_weights, [VMEM], weights, [],
        "sent_weights", 8, 2 * links * square * old, 2 * links * square,
    )(leaf_blocks)
    other = swap(sent, "sub", 1)
    own, parent_weight, leaf_table, parent_table = call(
        kept_weights, [VMEM] * 6,
        [weights, weights, shape((links, count), jnp.int32), shape((parent_links, half), jnp.int32)],
        [],
        "kept_weights", 8, 2 * (links + parent_links) * square * old, 8 * links * square,
    )(
        leaf_blocks, parent_blocks,
        leaf_partner_dev.T, leaf_partner_slot.T, parent_partner_group.T, parent_partner_slot.T,
    )
    tables = [
        pltpu.VMEM((8 * rank, 2 * rank), F32),
        pltpu.VMEM((8 * rank, 2 * rank), F32),
        pltpu.VMEM((8 * PANEL, 2 * rank), F32),
        pltpu.VMEM((half, 2 * rank, old), F32),
    ]
    change, stacked = call(
        leaf_step, [VMEM] * 6,
        [shape((2, half, rank, old), BF16), shape((half, 2, rank, old), F32)],
        tables, "leaf_step", 8, 40 * square * old, 8 * square,
    )(own, other, parent_weight, leaf_transfers, other_transfers, leaf_start)

    swapped = swap(change, "sub", 1)
    near = [swap(change, "sub", 2 * m) for m in range(1, chips)]
    parent_change = call(
        parent_step, [VMEM] * 3, shape((half, rank, old), BF16),
        tables, "parent_step", 8, 20 * square * old, 8 * square,
    )(parent_weight, stacked, parent_start)
    parents_held = [parent_change] + [
        swap(parent_change, "grp", m) for m in range(1, groups)
    ]
    token = shape((8, 128), F32)
    half_shape = shape((half, rank, links * old), BF16)
    own_bases, own_half, parent_half, after_middle = call(
        middle_own, [VMEM] * 6,
        [
            shape((half, rank, points), BF16), half_shape,
            shape((half, rank, parent_links * old), BF16), token,
        ],
        [pltpu.VMEM((4, rank, old), F32), pltpu.VMEM((4, rank, old), F32)],
        "middle_own", 8, 1 << 34, square,
    )(change, parent_change, leaf_bases, leaf_blocks, parent_blocks, swapped)
    packed = call(
        pack, [VMEM] * chips, shape((2 * chips - 2, half, rank, old), BF16), [],
        "pack", 4 + chips, 1 << 34, square,
    )(after_middle, *near)
    new_leaf_bases, other_half = call(
        middle_other, [VMEM] * 5, [shape((count, rank, points), BF16), half_shape],
        [pltpu.VMEM((4, rank, old), F32)],
        "middle_other", 8, square, square,
    )(swapped, leaf_bases, leaf_blocks, own_bases, packed)
    paused = call(pause, [VMEM], token, [], "pause", 4, 1 << 34, square)(packed)
    held = [change, swapped, *near, swap(packed, "sub", 1)]
    boxes = [(0,), (1,)] + [(2 * m,) for m in range(1, chips)]
    boxes += [tuple(2 * m + 1 for m in range(1, chips))]
    new_leaf_blocks, after_leaves = call(
        functools.partial(leaf_couple, boxes), [VMEM] * (4 + len(held)),
        [shape((count, links, rank * rank), BF16), token],
        [
            pltpu.VMEM((2 * chips * count, rank, old), BF16),
            pltpu.VMEM((4, 4 * rank, 2 * rank), F32),
        ],
        "leaf_couple", 4 + chips, 1 << 34, 12 * square,
    )(leaf_table, own_half, other_half, paused, *held)
    new_parent_blocks = call(
        parent_couple, [VMEM] * (groups + 3),
        shape((half, parent_links, rank * rank), BF16),
        [
            pltpu.VMEM((groups * half, rank, old), BF16),
            pltpu.VMEM((2, 4 * rank, 2 * rank), F32),
        ],
        "parent_couple", 4 + groups, square, 4 * square,
    )(parent_table, parent_half, after_leaves, *parents_held)
    return (new_leaf_bases, new_leaf_blocks, new_parent_blocks)


def solution(mesh):
    first = ("grp", "sub")
    placed = (
        P(first, None, None),
        P(first, None, None),
        P(first, None, None, None),
        P(first, None),
        P(first, None),
        P(first, None, None, None),
        P(first, None),
        P(first, None),
        P(),
        P(),
    )
    return jax.shard_map(
        shards,
        mesh=mesh,
        in_specs=placed,
        out_specs=(P(first, None, None),) * 3,
        check_vma=False,
    )
```

```python
import functools

import jax
import jax.numpy as jnp
from jax import lax
from jax.experimental import pallas as pl
from jax.experimental.pallas import tpu as pltpu
from jax.sharding import PartitionSpec as P

F32 = jnp.float32
BF16 = jnp.bfloat16
PIVOTS = 8
PANEL = 16
MIB = 1 << 20


def cat(parts, axis):
    return jnp.concatenate(parts, axis=axis)


def halves(value):
    high = value.astype(BF16)
    low = (value - high.astype(F32)).astype(BF16)
    return high, low


def dot(left, right):
    return lax.dot_general(left, right, (((1,), (0,)), ((), ())), preferred_element_type=F32)


def dot_t(left, right):
    return lax.dot_general(left, right, (((1,), (1,)), ((), ())), preferred_element_type=F32)


def fold(value):
    width = value.shape[1] // 2
    return value[:, :width] + value[:, width:]


def wide(value):
    return cat(halves(value), 1)


def tall(value):
    both = wide(value)
    return cat([both, both], 0)


def gram_sum(parts):
    row = cat(parts, 1)
    return dot_t(row, row)


def thirds(value):
    high, rest = halves_left(value)
    middle, rest = halves_left(rest)
    return high, middle, rest.astype(BF16)


def halves_left(value):
    high = value.astype(BF16)
    return high, value - high.astype(F32)


def eliminate(grid, made, turned, rank, pairs):
    shape = (8, 128)
    lane = lax.broadcasted_iota(jnp.int32, shape, 1)
    half = jnp.where(lane < rank, 0, rank)
    local = lane - half

    def spread(value, column):
        return jnp.take_along_axis(value, half + column, axis=1)

    for top in range(0, rank, PANEL):
        end = top + PANEL
        panel = [grid[8 * i : 8 * i + 8, :] for i in range(top, end)]
        for first in range(top, end, PIVOTS):
            last = first + PIVOTS
            rows = panel[first - top : last - top]
            corner = [[None] * PIVOTS for _ in range(PIVOTS)]
            for p in range(PIVOTS):
                for q in range(p, PIVOTS):
                    corner[p][q] = spread(rows[p], first + q)
            inside = (local >= first) & (local < last)
            rows = [
                jnp.where(inside, (local == first + p).astype(F32), rows[p])
                for p in range(PIVOTS)
            ]
            inverse = []
            for p in range(PIVOTS):
                inverse.append(1.0 / corner[p][p])
                for q in range(p + 1, PIVOTS):
                    factor = corner[p][q] * inverse[p]
                    for s in range(q, PIVOTS):
                        corner[q][s] = corner[q][s] - factor * corner[p][s]
                    rows[q] = rows[q] - factor * rows[p]
            scaled = [rows[p] * inverse[p] for p in range(PIVOTS)]
            for i in range(last, end):
                row = jnp.where(inside, 0.0, panel[i - top])
                for p in range(PIVOTS):
                    row = row - spread(scaled[p], i) * rows[p]
                panel[i - top] = row
            for p in range(PIVOTS):
                i = first + p
                done = jnp.where(local < last, rows[p] * lax.rsqrt(corner[p][p]), 0.0)
                made[8 * i : 8 * i + 8, :] = done
                if end < rank:
                    kept = rows[p]
                    if last < end:
                        kept = jnp.where((local < last) | (local >= end), kept, 0.0)
                    grid[8 * i : 8 * i + 8, :] = kept
                    at = 8 * (i - top)
                    turned[at : at + 8, :] = scaled[p]
        if end < rank:
            lane_below = lax.broadcasted_iota(jnp.int32, (rank - end, 2 * rank), 1)
            low = lane_below < rank
            local_below = lane_below - jnp.where(low, 0, rank)
            past = (local_below >= top) & (local_below < end)
            for pair in range(pairs):
                a, b, c = thirds(turned[pl.ds(pair, PANEL, stride=8), :])
                x, y, z = thirds(grid[pl.ds(8 * top + pair, PANEL, stride=8), :])
                full = lax.dot_general(
                    cat([a, a, a, b, b, c], 0), cat([x, y, z, x, y, x], 0),
                    (((0,), (0,)), ((), ())), preferred_element_type=F32,
                )
                full = jnp.where(low, full[end:rank], full[rank + end :])
                spot = pl.ds(8 * end + pair, rank - end, stride=8)
                grid[spot, :] = jnp.where(past, 0.0, grid[spot, :]) - full


def pair_rows(made, stored, pair, rank):
    wide_rank = 2 * rank
    factor = wide(made[pl.ds(pair, rank, stride=8), :])
    both = stored[pair]
    zero = jnp.zeros((rank, both.shape[1]), F32)
    spread = cat([cat([both[:rank], zero], 1), cat([zero, both[rank:]], 1)], 0)
    high, low = halves(spread)
    return dot(factor, cat([high, high], 0)) + dot(factor, cat([low, low], 0))


def store_gram(grid, stored, pair, images, rank):
    both = cat(images, 0)
    stored[pair] = both
    both_wide = wide(both)
    high, low = halves(both)
    full = dot_t(both_wide, cat([cat([high, high], 1), cat([low, low], 1)], 0))
    full = fold(full)
    lane = lax.broadcasted_iota(jnp.int32, (rank, 2 * rank), 1)
    grid[pl.ds(pair, rank, stride=8), :] = jnp.where(lane < rank, full[:rank], full[rank:])


def sent_weights(blocks, weight):
    half = weight.shape[0]
    start = (1 - lax.axis_index("sub") % 2) * half
    for j in range(half):
        weight[j] = gram_sum([blocks[start + j, c] for c in range(blocks.shape[1])])


def kept_weights(
    blocks, parents, devs, slots, groups, parent_slots, _,
    weight, parent_weight, leaf_table, parent_table,
):
    half = weight.shape[0]
    index = lax.axis_index("sub")
    member, chip = index & 1, index >> 1
    dev, slot = devs[...], slots[...]
    side = jnp.where(slot >= half, 1, 0)
    box = ((dev >> 1) ^ chip) * 2 + (side ^ member)
    leaf_table[...] = (box * 2 + ((dev & 1) ^ side)) * half + slot - side * half
    parent_table[...] = (groups[...] ^ lax.axis_index("grp")) * half + parent_slots[...]
    start = (lax.axis_index("sub") % 2) * half
    for j in range(half):
        weight[j] = gram_sum([blocks[start + j, c] for c in range(blocks.shape[1])])
        parent_weight[j] = gram_sum([parents[j, c] for c in range(parents.shape[1])])


def images_of(starts, weights):
    folded = [tall(weight) for weight in weights]
    images = [fold(dot(starts, each)) for each in folded]
    return [fold(dot(wide(image), each)) for image, each in zip(images, folded)]


def leaf_step(own, other, parent, transfers, other_transfers, start, change, stacked, grid, made, turned, stored):
    rank = start.shape[0]
    half = own.shape[0]
    member = lax.axis_index("sub") % 2
    first = member * half
    moves = [(transfers[first + j], other_transfers[first + j]) for j in range(half)]
    size = parent.shape[1]
    carried = [fold(dot(cat(moves[j], 0), wide(parent[j]))) for j in range(half)]
    weights = []
    for j in range(half):
        for at, base in enumerate((own[j], other[j])):
            part = wide(carried[j][at * size : at * size + size])
            weights.append(base + dot_t(part, cat([moves[j][at]] * 2, 1)))
    images = images_of(wide(start[...]), weights)
    for j in range(half):
        store_gram(grid, stored, j, images[2 * j : 2 * j + 2], rank)
    eliminate(grid, made, turned, rank, half)
    found = [pair_rows(made, stored, j, rank).astype(BF16) for j in range(half)]
    for j in range(half):
        width = found[j].shape[1] // 2
        mine, theirs = found[j][:, :width], found[j][:, width:]
        change[0, j] = mine
        change[1, j] = theirs
        stacked[j, member] = dot(mine, moves[j][0])
        stacked[j, 1 - member] = dot(theirs, moves[j][1])


def parent_step(parent, stacked, start, change, grid, made, turned, stored):
    rank = start.shape[0]
    half = parent.shape[0]
    rows = [cat([stacked[j, 0], stacked[j, 1]], 0) for j in range(half)]
    left = [fold(dot(wide(rows[j]), tall(parent[j]))) for j in range(half)]
    grams = []
    for j in range(half):
        high, low = halves(rows[j])
        right = cat([cat([high, high], 1), cat([low, low], 1)], 0)
        grams.append(fold(dot_t(wide(left[j]), right)))
    images = images_of(wide(start[...]), grams)
    for pair in range(half // 2):
        store_gram(grid, stored, pair, images[2 * pair : 2 * pair + 2], rank)
    eliminate(grid, made, turned, rank, half // 2)
    found = [pair_rows(made, stored, pair, rank) for pair in range(half // 2)]
    for j in range(half):
        width = found[0].shape[1] // 2
        at = j % 2 * width
        mixed = wide(found[j // 2][:, at : at + width])
        rows = tall(cat([stacked[j, 0], stacked[j, 1]], 0))
        change[j] = fold(dot(mixed, rows)).astype(BF16)


def parted(value, scratch):
    scratch[...] = value.astype(F32)
    count = value.shape[0] // 2
    return cat(
        [scratch[pl.ds(0, count, stride=2), :], scratch[pl.ds(1, count, stride=2), :]], 0
    ).astype(BF16)


def middle_own(
    change, parent_change, bases, blocks, parents, _,
    own_bases, own_half, parent_half, token,
    order, order_parents,
):
    token[...] = jnp.zeros(token.shape, token.dtype)
    half, links = parents.shape[0], blocks.shape[1]
    first = (lax.axis_index("sub") % 2) * half
    for j in range(half):
        rows = change[0, j]
        ordered = parted(rows, order.at[j % 4])
        own_bases[j] = dot_t(rows, bases[first + j]).astype(BF16)
        own_half[j] = dot(ordered, cat([blocks[first + j, c] for c in range(links)], 1)).astype(BF16)
    for j in range(half):
        ordered = parted(parent_change[j], order_parents.at[j % 4])
        parent_half[j] = dot(
            ordered, cat([parents[j, c] for c in range(parents.shape[1])], 1)
        ).astype(BF16)


def middle_other(swapped, bases, blocks, own_bases, _, new_bases, other_half, order):
    half, links = own_bases.shape[0], blocks.shape[1]
    member = lax.axis_index("sub") % 2
    first = (1 - member) * half
    new_bases[pl.ds(member * half, half)] = own_bases[...]
    for j in range(half):
        rows = swapped[1, j]
        ordered = parted(rows, order.at[j % 4])
        new_bases[first + j] = dot_t(rows, bases[first + j]).astype(BF16)
        other_half[j] = dot(
            ordered, cat([blocks[first + j, c] for c in range(links)], 1)
        ).astype(BF16)


def pack(*refs):
    _, *parts, out = refs
    count = parts[0].shape[0]
    for at, part in enumerate(parts):
        out[at * count : at * count + count] = part[...]


def pause(_, token):
    token[...] = jnp.zeros(token.shape, token.dtype)


def couple(middle, partner):
    full = dot_t(middle, partner)
    count = full.shape[0] // 2
    return cat([full[:count], full[count:]], 1)


def write_rows(out, at, order, links, count):
    for m in range(count):
        out[at, :, m * 128 : m * 128 + 128] = order[8 * m : 8 * m + links, :].astype(BF16)


def leaf_couple(boxes, table_in, own_half, other_half, _, *rest):
    held_boxes, (out, token, held, order) = rest[:-4], rest[-4:]
    table = table_in[...]
    count, links = out.shape[0], out.shape[1]
    half, rank = own_half.shape[:2]
    member = lax.axis_index("sub") % 2
    token[...] = jnp.zeros(token.shape, token.dtype)
    size = 2 * held_boxes[0].shape[1]
    for box, source in zip(boxes, held_boxes):
        for at, place in enumerate(box):
            part = source[2 * at : 2 * at + 2]
            held[place * size : place * size + size] = part.reshape((size,) + part.shape[2:])
    for at in range(count):
        own = at < half
        middle = own_half if own else other_half
        j = at % half
        t = (member if own else 1 - member) * half + j
        rows = jnp.where(member == (0 if own else 1), table[:, j : j + 1], table[:, half + j : half + j + 1])
        for c in range(links):
            order[at % 4, pl.ds(c, rank // 2, stride=8), :] = couple(
                middle[j, :, c * 128 : c * 128 + 128], held[rows[c, 0]]
            )
        write_rows(out, t, order.at[at % 4], links, rank // 2)


def parent_couple(table_in, middle, _, *rest):
    near, (out, held, order) = rest[:-3], rest[-3:]
    table = table_in[...]
    count, links = out.shape[0], out.shape[1]
    rank = middle.shape[1]
    for m in range(len(near)):
        held[m * count : m * count + count] = near[m][...]
    for p in range(count):
        for c in range(links):
            order[p % 2, pl.ds(c, rank // 2, stride=8), :] = couple(
                middle[p, :, c * 128 : c * 128 + 128], held[table[c, p]]
            )
        write_rows(out, p, order.at[p % 2], links, rank // 2)


VMEM = pl.BlockSpec(memory_space=pltpu.VMEM)
ANY = pl.BlockSpec(memory_space=pl.ANY)
HBM = pl.BlockSpec(memory_space=pltpu.HBM)


def call(body, ins, out_shapes, scratch, name, mib, flops, moved):
    many = isinstance(out_shapes, list)
    return pl.pallas_call(
        body,
        out_shape=out_shapes,
        in_specs=ins,
        out_specs=[VMEM] * len(out_shapes) if many else VMEM,
        scratch_shapes=scratch,
        name=name,
        compiler_params=pltpu.CompilerParams(vmem_limit_bytes=mib * MIB),
        cost_estimate=pl.CostEstimate(flops=flops, bytes_accessed=moved, transcendentals=0),
    )


def swap(block, axis, mask):
    count = lax.axis_size(axis)
    return lax.ppermute(block, axis, [(i, i ^ mask) for i in range(count)])


def shards(
    leaf_bases,
    leaf_transfers,
    leaf_blocks,
    leaf_partner_dev,
    leaf_partner_slot,
    parent_blocks,
    parent_partner_group,
    parent_partner_slot,
    leaf_start,
    parent_start,
):
    count, links, old = leaf_blocks.shape[:3]
    half, parent_links = parent_blocks.shape[:2]
    rank = leaf_start.shape[0]
    points = leaf_bases.shape[1]
    chips = lax.axis_size("sub") // 2
    groups = lax.axis_size("grp")
    shape = jax.ShapeDtypeStruct
    dma = pltpu.SemaphoreType.DMA
    square = half * old * old

    weights = shape((half, old, old), F32)
    other_transfers = swap(leaf_transfers, "sub", 1)
    sent = call(
        sent_weights, [VMEM], weights, [],
        "sent_weights", 8, 2 * links * square * old, 2 * links * square,
    )(leaf_blocks)
    other = swap(sent, "sub", 1)
    own, parent_weight, leaf_table, parent_table = call(
        kept_weights, [VMEM] * 7,
        [weights, weights, shape((links, count), jnp.int32), shape((parent_links, half), jnp.int32)],
        [],
        "kept_weights", 8, 2 * (links + parent_links) * square * old, 8 * links * square,
    )(
        leaf_blocks, parent_blocks,
        leaf_partner_dev.T, leaf_partner_slot.T, parent_partner_group.T, parent_partner_slot.T,
        other_transfers,
    )
    tables = [
        pltpu.VMEM((8 * rank, 2 * rank), F32),
        pltpu.VMEM((8 * rank, 2 * rank), F32),
        pltpu.VMEM((8 * PANEL, 2 * rank), F32),
        pltpu.VMEM((half, 2 * rank, old), F32),
    ]
    change, stacked = call(
        leaf_step, [VMEM] * 6,
        [shape((2, half, rank, old), BF16), shape((half, 2, rank, old), F32)],
        tables, "leaf_step", 8, 40 * square * old, 8 * square,
    )(own, other, parent_weight, leaf_transfers, other_transfers, leaf_start)

    swapped = swap(change, "sub", 1)
    near = [swap(change, "sub", 2 * m) for m in range(1, chips)]
    parent_change = call(
        parent_step, [VMEM] * 3, shape((half, rank, old), BF16),
        tables, "parent_step", 8, 20 * square * old, 8 * square,
    )(parent_weight, stacked, parent_start)
    parents_held = [parent_change] + [
        swap(parent_change, "grp", m) for m in range(1, groups)
    ]
    token = shape((8, 128), F32)
    half_shape = shape((half, rank, links * old), BF16)
    own_bases, own_half, parent_half, after_middle = call(
        middle_own, [VMEM] * 6,
        [
            shape((half, rank, points), BF16), half_shape,
            shape((half, rank, parent_links * old), BF16), token,
        ],
        [pltpu.VMEM((4, rank, old), F32), pltpu.VMEM((4, rank, old), F32)],
        "middle_own", 8, 1 << 34, square,
    )(change, parent_change, leaf_bases, leaf_blocks, parent_blocks, swapped)
    packed = call(
        pack, [VMEM] * chips, shape((2 * chips - 2, half, rank, old), BF16), [],
        "pack", 4 + chips, 1 << 34, square,
    )(after_middle, *near)
    new_leaf_bases, other_half = call(
        middle_other, [VMEM] * 5, [shape((count, rank, points), BF16), half_shape],
        [pltpu.VMEM((4, rank, old), F32)],
        "middle_other", 8, square, square,
    )(swapped, leaf_bases, leaf_blocks, own_bases, packed)
    paused = call(pause, [VMEM], token, [], "pause", 4, 1 << 34, square)(packed)
    held = [change, swapped, *near, swap(packed, "sub", 1)]
    boxes = [(0,), (1,)] + [(2 * m,) for m in range(1, chips)]
    boxes += [tuple(2 * m + 1 for m in range(1, chips))]
    new_leaf_blocks, after_leaves = call(
        functools.partial(leaf_couple, boxes), [VMEM] * (4 + len(held)),
        [shape((count, links, rank * rank), BF16), token],
        [
            pltpu.VMEM((2 * chips * count, rank, old), BF16),
            pltpu.VMEM((4, 4 * rank, 2 * rank), F32),
        ],
        "leaf_couple", 4 + chips, 1 << 34, 12 * square,
    )(leaf_table, own_half, other_half, paused, *held)
    new_parent_blocks = call(
        parent_couple, [VMEM] * (groups + 3),
        shape((half, parent_links, rank * rank), BF16),
        [
            pltpu.VMEM((groups * half, rank, old), BF16),
            pltpu.VMEM((2, 4 * rank, 2 * rank), F32),
        ],
        "parent_couple", 4 + groups, square, 4 * square,
    )(parent_table, parent_half, after_leaves, *parents_held)
    return (new_leaf_bases, new_leaf_blocks, new_parent_blocks)


def solution(mesh):
    first = ("grp", "sub")
    placed = (
        P(first, None, None),
        P(first, None, None),
        P(first, None, None, None),
        P(first, None),
        P(first, None),
        P(first, None, None, None),
        P(first, None),
        P(first, None),
        P(),
        P(),
    )
    return jax.shard_map(
        shards,
        mesh=mesh,
        in_specs=placed,
        out_specs=(P(first, None, None),) * 3,
        check_vma=False,
    )
```

```python
import functools

import jax
import jax.numpy as jnp
from jax import lax
from jax.experimental import pallas as pl
from jax.experimental.pallas import tpu as pltpu
from jax.sharding import PartitionSpec as P

F32 = jnp.float32
BF16 = jnp.bfloat16
PIVOTS = 8
PANEL = 16
MIB = 1 << 20


def cat(parts, axis):
    return jnp.concatenate(parts, axis=axis)


def halves(value):
    high = value.astype(BF16)
    low = (value - high.astype(F32)).astype(BF16)
    return high, low


def dot(left, right):
    return lax.dot_general(left, right, (((1,), (0,)), ((), ())), preferred_element_type=F32)


def dot_t(left, right):
    return lax.dot_general(left, right, (((1,), (1,)), ((), ())), preferred_element_type=F32)


def fold(value):
    width = value.shape[1] // 2
    return value[:, :width] + value[:, width:]


def wide(value):
    return cat(halves(value), 1)


def tall(value):
    both = wide(value)
    return cat([both, both], 0)


def gram_sum(parts):
    row = cat(parts, 1)
    return dot_t(row, row)


def thirds(value):
    high, rest = halves_left(value)
    middle, rest = halves_left(rest)
    return high, middle, rest.astype(BF16)


def halves_left(value):
    high = value.astype(BF16)
    return high, value - high.astype(F32)


def eliminate(grid, made, turned, rank, pairs):
    shape = (8, 128)
    lane = lax.broadcasted_iota(jnp.int32, shape, 1)
    half = jnp.where(lane < rank, 0, rank)
    local = lane - half

    def spread(value, column):
        return jnp.take_along_axis(value, half + column, axis=1)

    for top in range(0, rank, PANEL):
        end = top + PANEL
        panel = [grid[8 * i : 8 * i + 8, :] for i in range(top, end)]
        for first in range(top, end, PIVOTS):
            last = first + PIVOTS
            rows = panel[first - top : last - top]
            corner = [[None] * PIVOTS for _ in range(PIVOTS)]
            for p in range(PIVOTS):
                for q in range(p, PIVOTS):
                    corner[p][q] = spread(rows[p], first + q)
            inside = (local >= first) & (local < last)
            rows = [
                jnp.where(inside, (local == first + p).astype(F32), rows[p])
                for p in range(PIVOTS)
            ]
            inverse = []
            for p in range(PIVOTS):
                inverse.append(1.0 / corner[p][p])
                for q in range(p + 1, PIVOTS):
                    factor = corner[p][q] * inverse[p]
                    for s in range(q, PIVOTS):
                        corner[q][s] = corner[q][s] - factor * corner[p][s]
                    rows[q] = rows[q] - factor * rows[p]
            scaled = [rows[p] * inverse[p] for p in range(PIVOTS)]
            for i in range(last, end):
                row = jnp.where(inside, 0.0, panel[i - top])
                for p in range(PIVOTS):
                    row = row - spread(scaled[p], i) * rows[p]
                panel[i - top] = row
            for p in range(PIVOTS):
                i = first + p
                done = jnp.where(local < last, rows[p] * lax.rsqrt(corner[p][p]), 0.0)
                made[8 * i : 8 * i + 8, :] = done
                if end < rank:
                    kept = rows[p]
                    if last < end:
                        kept = jnp.where((local < last) | (local >= end), kept, 0.0)
                    grid[8 * i : 8 * i + 8, :] = kept
                    at = 8 * (i - top)
                    turned[at : at + 8, :] = scaled[p]
        if end < rank:
            lane_below = lax.broadcasted_iota(jnp.int32, (rank - end, 2 * rank), 1)
            low = lane_below < rank
            local_below = lane_below - jnp.where(low, 0, rank)
            past = (local_below >= top) & (local_below < end)
            for pair in range(pairs):
                a, b, c = thirds(turned[pl.ds(pair, PANEL, stride=8), :])
                x, y, z = thirds(grid[pl.ds(8 * top + pair, PANEL, stride=8), :])
                full = lax.dot_general(
                    cat([a, a, a, b, b, c], 0), cat([x, y, z, x, y, x], 0),
                    (((0,), (0,)), ((), ())), preferred_element_type=F32,
                )
                full = jnp.where(low, full[end:rank], full[rank + end :])
                spot = pl.ds(8 * end + pair, rank - end, stride=8)
                grid[spot, :] = jnp.where(past, 0.0, grid[spot, :]) - full


def pair_rows(made, stored, pair, rank):
    wide_rank = 2 * rank
    factor = wide(made[pl.ds(pair, rank, stride=8), :])
    both = stored[pair]
    zero = jnp.zeros((rank, both.shape[1]), F32)
    spread = cat([cat([both[:rank], zero], 1), cat([zero, both[rank:]], 1)], 0)
    high, low = halves(spread)
    return dot(factor, cat([high, high], 0)) + dot(factor, cat([low, low], 0))


def store_gram(grid, stored, pair, images, rank):
    both = cat(images, 0)
    stored[pair] = both
    both_wide = wide(both)
    high, low = halves(both)
    full = dot_t(both_wide, cat([cat([high, high], 1), cat([low, low], 1)], 0))
    full = fold(full)
    lane = lax.broadcasted_iota(jnp.int32, (rank, 2 * rank), 1)
    grid[pl.ds(pair, rank, stride=8), :] = jnp.where(lane < rank, full[:rank], full[rank:])


def sent_weights(blocks, weight):
    half = weight.shape[0]
    start = (1 - lax.axis_index("sub") % 2) * half
    for j in range(half):
        weight[j] = gram_sum([blocks[start + j, c] for c in range(blocks.shape[1])])


def kept_weights(
    order, blocks, parents, devs, slots, groups, parent_slots, transfers, start_rows, _,
    own_images, parent_weight, leaf_table, parent_table,
):
    half = own_images.shape[0]
    index = lax.axis_index("sub")
    member, chip = index & 1, index >> 1
    dev, slot = devs[...], slots[...]
    side = jnp.where(slot >= half, 1, 0)
    box = ((dev >> 1) ^ chip) * 2 + (side ^ member)
    leaf_table[...] = (box * 2 + ((dev & 1) ^ side)) * half + slot - side * half
    apart = groups[...] ^ lax.axis_index("grp")
    place = jnp.zeros_like(apart)
    for at, mask in enumerate(order):
        place = jnp.where(apart == mask, at, place)
    parent_table[...] = place * half + parent_slots[...]
    start = member * half
    weights = []
    for j in range(half):
        parent_weight[j] = gram_sum([parents[j, c] for c in range(parents.shape[1])])
        weights.append(gram_sum([blocks[start + j, c] for c in range(blocks.shape[1])]))
    moves = [transfers[start + j] for j in range(half)]
    weights = descend(weights, moves, [parent_weight[j] for j in range(half)])
    for j, image in enumerate(images_of(wide(start_rows[...]), weights)):
        own_images[j] = image


def descend(weights, moves, parents):
    carried = [fold(dot(move, wide(parent))) for move, parent in zip(moves, parents)]
    return [
        weight + dot_t(wide(part), cat([move, move], 1))
        for weight, part, move in zip(weights, carried, moves)
    ]


def images_of(starts, weights):
    folded = [tall(weight) for weight in weights]
    images = [fold(dot(starts, each)) for each in folded]
    return [fold(dot(wide(image), each)) for image, each in zip(images, folded)]


def leaf_step(
    own_images, other, parent, transfers, other_transfers, start, change, stacked,
    grid, made, turned, stored,
):
    rank = start.shape[0]
    half = other.shape[0]
    member = lax.axis_index("sub") % 2
    first = member * half
    moves = [(transfers[first + j], other_transfers[first + j]) for j in range(half)]
    weights = descend(
        [other[j] for j in range(half)], [move for _, move in moves], [parent[j] for j in range(half)]
    )
    others = images_of(wide(start[...]), weights)
    for j in range(half):
        store_gram(grid, stored, j, [own_images[j], others[j]], rank)
    eliminate(grid, made, turned, rank, half)
    found = [pair_rows(made, stored, j, rank).astype(BF16) for j in range(half)]
    for j in range(half):
        width = found[j].shape[1] // 2
        mine, theirs = found[j][:, :width], found[j][:, width:]
        change[0, j] = mine
        change[1, j] = theirs
        stacked[j, member] = dot(mine, moves[j][0])
        stacked[j, 1 - member] = dot(theirs, moves[j][1])


def parent_step(parent, stacked, start, change, grid, made, turned, stored):
    rank = start.shape[0]
    half = parent.shape[0]
    rows = [cat([stacked[j, 0], stacked[j, 1]], 0) for j in range(half)]
    left = [fold(dot(wide(rows[j]), tall(parent[j]))) for j in range(half)]
    grams = []
    for j in range(half):
        high, low = halves(rows[j])
        right = cat([cat([high, high], 1), cat([low, low], 1)], 0)
        grams.append(fold(dot_t(wide(left[j]), right)))
    images = images_of(wide(start[...]), grams)
    for pair in range(half // 2):
        store_gram(grid, stored, pair, images[2 * pair : 2 * pair + 2], rank)
    eliminate(grid, made, turned, rank, half // 2)
    found = [pair_rows(made, stored, pair, rank) for pair in range(half // 2)]
    for j in range(half):
        width = found[0].shape[1] // 2
        at = j % 2 * width
        mixed = wide(found[j // 2][:, at : at + width])
        rows = tall(cat([stacked[j, 0], stacked[j, 1]], 0))
        change[j] = fold(dot(mixed, rows)).astype(BF16)


def parted(value, scratch):
    scratch[...] = value.astype(F32)
    count = value.shape[0] // 2
    return cat(
        [scratch[pl.ds(0, count, stride=2), :], scratch[pl.ds(1, count, stride=2), :]], 0
    ).astype(BF16)


def middle_own(
    change, parent_change, bases, blocks, parents, _,
    own_bases, own_half, parent_half, token,
    order, order_parents,
):
    token[...] = jnp.zeros(token.shape, token.dtype)
    half, links = parents.shape[0], blocks.shape[1]
    first = (lax.axis_index("sub") % 2) * half
    for j in range(half):
        rows = change[0, j]
        ordered = parted(rows, order.at[j % 4])
        own_bases[j] = dot_t(rows, bases[first + j]).astype(BF16)
        own_half[j] = dot(ordered, cat([blocks[first + j, c] for c in range(links)], 1)).astype(BF16)
    for j in range(half):
        ordered = parted(parent_change[j], order_parents.at[j % 4])
        parent_half[j] = dot(
            ordered, cat([parents[j, c] for c in range(parents.shape[1])], 1)
        ).astype(BF16)


def middle_other(swapped, bases, blocks, own_bases, _, new_bases, other_half, order):
    half, links = own_bases.shape[0], blocks.shape[1]
    member = lax.axis_index("sub") % 2
    first = (1 - member) * half
    new_bases[pl.ds(member * half, half)] = own_bases[...]
    for j in range(half):
        rows = swapped[1, j]
        ordered = parted(rows, order.at[j % 4])
        new_bases[first + j] = dot_t(rows, bases[first + j]).astype(BF16)
        other_half[j] = dot(
            ordered, cat([blocks[first + j, c] for c in range(links)], 1)
        ).astype(BF16)


def pack(*refs):
    _, *parts, out = refs
    count = parts[0].shape[0]
    for at, part in enumerate(parts):
        out[at * count : at * count + count] = part[...]


def pause(_, token):
    token[...] = jnp.zeros(token.shape, token.dtype)


def couple(middle, partner):
    full = dot_t(middle, partner)
    count = full.shape[0] // 2
    return cat([full[:count], full[count:]], 1)


def write_rows(out, at, order, links, count):
    for m in range(count):
        out[at, :, m * 128 : m * 128 + 128] = order[8 * m : 8 * m + links, :].astype(BF16)


def leaf_couple(boxes, table_in, own_half, other_half, _, *rest):
    held_boxes, (out, token, held, order) = rest[:-4], rest[-4:]
    table = table_in[...]
    count, links = out.shape[0], out.shape[1]
    half, rank = own_half.shape[:2]
    member = lax.axis_index("sub") % 2
    token[...] = jnp.zeros(token.shape, token.dtype)
    size = 2 * held_boxes[0].shape[1]
    for box, source in zip(boxes, held_boxes):
        for at, place in enumerate(box):
            part = source[2 * at : 2 * at + 2]
            held[place * size : place * size + size] = part.reshape((size,) + part.shape[2:])
    for at in range(count):
        own = at < half
        middle = own_half if own else other_half
        j = at % half
        t = (member if own else 1 - member) * half + j
        rows = jnp.where(member == (0 if own else 1), table[:, j : j + 1], table[:, half + j : half + j + 1])
        for c in range(links):
            order[at % 4, pl.ds(c, rank // 2, stride=8), :] = couple(
                middle[j, :, c * 128 : c * 128 + 128], held[rows[c, 0]]
            )
        write_rows(out, t, order.at[at % 4], links, rank // 2)


def parent_couple(table_in, middle, _, *rest):
    near, (out, held, order) = rest[:-3], rest[-3:]
    table = table_in[...]
    count, links = out.shape[0], out.shape[1]
    rank = middle.shape[1]
    for m in range(len(near)):
        held[m * count : m * count + count] = near[m][...]
    for p in range(count):
        for c in range(links):
            order[p % 2, pl.ds(c, rank // 2, stride=8), :] = couple(
                middle[p, :, c * 128 : c * 128 + 128], held[table[c, p]]
            )
        write_rows(out, p, order.at[p % 2], links, rank // 2)


VMEM = pl.BlockSpec(memory_space=pltpu.VMEM)
ANY = pl.BlockSpec(memory_space=pl.ANY)
HBM = pl.BlockSpec(memory_space=pltpu.HBM)


def call(body, ins, out_shapes, scratch, name, mib, flops, moved):
    many = isinstance(out_shapes, list)
    return pl.pallas_call(
        body,
        out_shape=out_shapes,
        in_specs=ins,
        out_specs=[VMEM] * len(out_shapes) if many else VMEM,
        scratch_shapes=scratch,
        name=name,
        compiler_params=pltpu.CompilerParams(vmem_limit_bytes=mib * MIB),
        cost_estimate=pl.CostEstimate(flops=flops, bytes_accessed=moved, transcendentals=0),
    )


def swap(block, axis, mask):
    count = lax.axis_size(axis)
    return lax.ppermute(block, axis, [(i, i ^ mask) for i in range(count)])


def group_order(groups):
    return (0, 2, 3, 1) if groups == 4 else tuple(range(groups))


def shards(
    leaf_bases,
    leaf_transfers,
    leaf_blocks,
    leaf_partner_dev,
    leaf_partner_slot,
    parent_blocks,
    parent_partner_group,
    parent_partner_slot,
    leaf_start,
    parent_start,
):
    count, links, old = leaf_blocks.shape[:3]
    half, parent_links = parent_blocks.shape[:2]
    rank = leaf_start.shape[0]
    points = leaf_bases.shape[1]
    chips = lax.axis_size("sub") // 2
    groups = lax.axis_size("grp")
    shape = jax.ShapeDtypeStruct
    dma = pltpu.SemaphoreType.DMA
    square = half * old * old

    weights = shape((half, old, old), F32)
    other_transfers = swap(leaf_transfers, "sub", 1)
    sent = call(
        sent_weights, [VMEM], weights, [],
        "sent_weights", 8, 2 * links * square * old, 2 * links * square,
    )(leaf_blocks)
    other = swap(sent, "sub", 1)
    order = group_order(groups)
    own, parent_weight, leaf_table, parent_table = call(
        functools.partial(kept_weights, order), [VMEM] * 9,
        [shape((half, rank, old), F32), weights, shape((links, count), jnp.int32), shape((parent_links, half), jnp.int32)],
        [],
        "kept_weights", 8, 2 * (links + parent_links) * square * old, 8 * links * square,
    )(
        leaf_blocks, parent_blocks,
        leaf_partner_dev.T, leaf_partner_slot.T, parent_partner_group.T, parent_partner_slot.T,
        leaf_transfers, leaf_start, other_transfers,
    )
    tables = [
        pltpu.VMEM((8 * rank, 2 * rank), F32),
        pltpu.VMEM((8 * rank, 2 * rank), F32),
        pltpu.VMEM((8 * PANEL, 2 * rank), F32),
        pltpu.VMEM((half, 2 * rank, old), F32),
    ]
    change, stacked = call(
        leaf_step, [VMEM] * 6,
        [shape((2, half, rank, old), BF16), shape((half, 2, rank, old), F32)],
        tables, "leaf_step", 8, 40 * square * old, 8 * square,
    )(own, other, parent_weight, leaf_transfers, other_transfers, leaf_start)

    swapped = swap(change, "sub", 1)
    near = [swap(change, "sub", 2 * m) for m in range(1, chips)]
    parent_change = call(
        parent_step, [VMEM] * 3, shape((half, rank, old), BF16),
        tables, "parent_step", 8, 20 * square * old, 8 * square,
    )(parent_weight, stacked, parent_start)
    parents_held = [parent_change] + [
        swap(parent_change, "grp", m) for m in order[1:]
    ]
    token = shape((8, 128), F32)
    half_shape = shape((half, rank, links * old), BF16)
    own_bases, own_half, parent_half, after_middle = call(
        middle_own, [VMEM] * 6,
        [
            shape((half, rank, points), BF16), half_shape,
            shape((half, rank, parent_links * old), BF16), token,
        ],
        [pltpu.VMEM((4, rank, old), F32), pltpu.VMEM((4, rank, old), F32)],
        "middle_own", 8, 1 << 34, square,
    )(change, parent_change, leaf_bases, leaf_blocks, parent_blocks, swapped)
    packed = call(
        pack, [VMEM] * chips, shape((2 * chips - 2, half, rank, old), BF16), [],
        "pack", 4 + chips, 1 << 34, square,
    )(after_middle, *near)
    new_leaf_bases, other_half = call(
        middle_other, [VMEM] * 5, [shape((count, rank, points), BF16), half_shape],
        [pltpu.VMEM((4, rank, old), F32)],
        "middle_other", 8, square, square,
    )(swapped, leaf_bases, leaf_blocks, own_bases, packed)
    paused = call(pause, [VMEM], token, [], "pause", 4, 1 << 34, square)(packed)
    held = [change, swapped, *near, swap(packed, "sub", 1)]
    boxes = [(0,), (1,)] + [(2 * m,) for m in range(1, chips)]
    boxes += [tuple(2 * m + 1 for m in range(1, chips))]
    new_leaf_blocks, after_leaves = call(
        functools.partial(leaf_couple, boxes), [VMEM] * (4 + len(held)),
        [shape((count, links, rank * rank), BF16), token],
        [
            pltpu.VMEM((2 * chips * count, rank, old), BF16),
            pltpu.VMEM((4, 4 * rank, 2 * rank), F32),
        ],
        "leaf_couple", 4 + chips, 1 << 34, 12 * square,
    )(leaf_table, own_half, other_half, paused, *held)
    new_parent_blocks = call(
        parent_couple, [VMEM] * (groups + 3),
        shape((half, parent_links, rank * rank), BF16),
        [
            pltpu.VMEM((groups * half, rank, old), BF16),
            pltpu.VMEM((2, 4 * rank, 2 * rank), F32),
        ],
        "parent_couple", 4 + groups, square, 4 * square,
    )(parent_table, parent_half, after_leaves, *parents_held)
    return (new_leaf_bases, new_leaf_blocks, new_parent_blocks)


def solution(mesh):
    first = ("grp", "sub")
    placed = (
        P(first, None, None),
        P(first, None, None),
        P(first, None, None, None),
        P(first, None),
        P(first, None),
        P(first, None, None, None),
        P(first, None),
        P(first, None),
        P(),
        P(),
    )
    return jax.shard_map(
        shards,
        mesh=mesh,
        in_specs=placed,
        out_specs=(P(first, None, None),) * 3,
        check_vma=False,
    )
```

```python
import functools

import jax
import jax.numpy as jnp
from jax import lax
from jax.experimental import pallas as pl
from jax.experimental.pallas import tpu as pltpu
from jax.sharding import PartitionSpec as P

F32 = jnp.float32
BF16 = jnp.bfloat16
PIVOTS = 8
PANEL = 16
MIB = 1 << 20


def cat(parts, axis):
    return jnp.concatenate(parts, axis=axis)


def halves(value):
    high = value.astype(BF16)
    low = (value - high.astype(F32)).astype(BF16)
    return high, low


def dot(left, right):
    return lax.dot_general(left, right, (((1,), (0,)), ((), ())), preferred_element_type=F32)


def dot_t(left, right):
    return lax.dot_general(left, right, (((1,), (1,)), ((), ())), preferred_element_type=F32)


def fold(value):
    width = value.shape[1] // 2
    return value[:, :width] + value[:, width:]


def wide(value):
    return cat(halves(value), 1)


def tall(value):
    both = wide(value)
    return cat([both, both], 0)


def gram_sum(parts):
    row = cat(parts, 1)
    return dot_t(row, row)


def thirds(value):
    high, rest = halves_left(value)
    middle, rest = halves_left(rest)
    return high, middle, rest.astype(BF16)


def halves_left(value):
    high = value.astype(BF16)
    return high, value - high.astype(F32)


def eliminate(grid, made, turned, rank, pairs):
    shape = (8, 128)
    lane = lax.broadcasted_iota(jnp.int32, shape, 1)
    half = jnp.where(lane < rank, 0, rank)
    local = lane - half

    def spread(value, column):
        return jnp.take_along_axis(value, half + column, axis=1)

    for top in range(0, rank, PANEL):
        end = top + PANEL
        panel = [grid[8 * i : 8 * i + 8, :] for i in range(top, end)]
        for first in range(top, end, PIVOTS):
            last = first + PIVOTS
            rows = panel[first - top : last - top]
            corner = [[None] * PIVOTS for _ in range(PIVOTS)]
            for p in range(PIVOTS):
                for q in range(p, PIVOTS):
                    corner[p][q] = spread(rows[p], first + q)
            inside = (local >= first) & (local < last)
            rows = [
                jnp.where(inside, (local == first + p).astype(F32), rows[p])
                for p in range(PIVOTS)
            ]
            inverse = []
            for p in range(PIVOTS):
                inverse.append(1.0 / corner[p][p])
                for q in range(p + 1, PIVOTS):
                    factor = corner[p][q] * inverse[p]
                    for s in range(q, PIVOTS):
                        corner[q][s] = corner[q][s] - factor * corner[p][s]
                    rows[q] = rows[q] - factor * rows[p]
            scaled = [rows[p] * inverse[p] for p in range(PIVOTS)]
            for i in range(last, end):
                row = jnp.where(inside, 0.0, panel[i - top])
                for p in range(PIVOTS):
                    row = row - spread(scaled[p], i) * rows[p]
                panel[i - top] = row
            for p in range(PIVOTS):
                i = first + p
                done = jnp.where(local < last, rows[p] * lax.rsqrt(corner[p][p]), 0.0)
                made[8 * i : 8 * i + 8, :] = done
                if end < rank:
                    kept = rows[p]
                    if last < end:
                        kept = jnp.where((local < last) | (local >= end), kept, 0.0)
                    grid[8 * i : 8 * i + 8, :] = kept
                    at = 8 * (i - top)
                    turned[at : at + 8, :] = scaled[p]
        if end < rank:
            lane_below = lax.broadcasted_iota(jnp.int32, (rank - end, 2 * rank), 1)
            low = lane_below < rank
            local_below = lane_below - jnp.where(low, 0, rank)
            past = (local_below >= top) & (local_below < end)
            for pair in range(pairs):
                a, b, c = thirds(turned[pl.ds(pair, PANEL, stride=8), :])
                x, y, z = thirds(grid[pl.ds(8 * top + pair, PANEL, stride=8), :])
                full = lax.dot_general(
                    cat([a, a, a, b, b, c], 0), cat([x, y, z, x, y, x], 0),
                    (((0,), (0,)), ((), ())), preferred_element_type=F32,
                )
                full = jnp.where(low, full[end:rank], full[rank + end :])
                spot = pl.ds(8 * end + pair, rank - end, stride=8)
                grid[spot, :] = jnp.where(past, 0.0, grid[spot, :]) - full


def pair_rows(made, stored, pair, rank):
    wide_rank = 2 * rank
    factor = wide(made[pl.ds(pair, rank, stride=8), :])
    both = stored[pair]
    zero = jnp.zeros((rank, both.shape[1]), F32)
    spread = cat([cat([both[:rank], zero], 1), cat([zero, both[rank:]], 1)], 0)
    high, low = halves(spread)
    return dot(factor, cat([high, high], 0)) + dot(factor, cat([low, low], 0))


def store_gram(grid, stored, pair, images, rank):
    both = cat(images, 0)
    stored[pair] = both
    both_wide = wide(both)
    high, low = halves(both)
    full = dot_t(both_wide, cat([cat([high, high], 1), cat([low, low], 1)], 0))
    full = fold(full)
    lane = lax.broadcasted_iota(jnp.int32, (rank, 2 * rank), 1)
    grid[pl.ds(pair, rank, stride=8), :] = jnp.where(lane < rank, full[:rank], full[rank:])


def sent_weights(blocks, weight):
    half = weight.shape[0]
    start = (1 - lax.axis_index("sub") % 2) * half
    for j in range(half):
        weight[j] = gram_sum([blocks[start + j, c] for c in range(blocks.shape[1])])


def kept_weights(
    order, blocks, parents, devs, slots, groups, parent_slots, transfers, start_rows, _,
    own_images, parent_weight, leaf_table, parent_table,
):
    half = own_images.shape[0]
    index = lax.axis_index("sub")
    member, chip = index & 1, index >> 1
    dev, slot = devs[...], slots[...]
    side = jnp.where(slot >= half, 1, 0)
    box = ((dev >> 1) ^ chip) * 2 + (side ^ member)
    leaf_table[...] = (box * 2 + ((dev & 1) ^ side)) * half + slot - side * half
    apart = groups[...] ^ lax.axis_index("grp")
    place = jnp.zeros_like(apart)
    for at, mask in enumerate(order):
        place = jnp.where(apart == mask, at, place)
    parent_table[...] = place * half + parent_slots[...]
    start = member * half
    weights = []
    for j in range(half):
        parent_weight[j] = gram_sum([parents[j, c] for c in range(parents.shape[1])])
        weights.append(gram_sum([blocks[start + j, c] for c in range(blocks.shape[1])]))
    moves = [transfers[start + j] for j in range(half)]
    weights = descend(weights, moves, [parent_weight[j] for j in range(half)])
    for j, image in enumerate(images_of(wide(start_rows[...]), weights)):
        own_images[j] = image


def descend(weights, moves, parents):
    carried = [fold(dot(move, wide(parent))) for move, parent in zip(moves, parents)]
    return [
        weight + dot_t(wide(part), cat([move, move], 1))
        for weight, part, move in zip(weights, carried, moves)
    ]


def images_of(starts, weights):
    folded = [tall(weight) for weight in weights]
    images = [fold(dot(starts, each)) for each in folded]
    return [fold(dot(wide(image), each)) for image, each in zip(images, folded)]


def leaf_step(
    own_images, other, parent, transfers, other_transfers, start, change, stacked,
    grid, made, turned, stored,
):
    rank = start.shape[0]
    half = other.shape[0]
    member = lax.axis_index("sub") % 2
    first = member * half
    moves = [(transfers[first + j], other_transfers[first + j]) for j in range(half)]
    weights = descend(
        [other[j] for j in range(half)], [move for _, move in moves], [parent[j] for j in range(half)]
    )
    others = images_of(wide(start[...]), weights)
    for j in range(half):
        store_gram(grid, stored, j, [own_images[j], others[j]], rank)
    eliminate(grid, made, turned, rank, half)
    found = [pair_rows(made, stored, j, rank).astype(BF16) for j in range(half)]
    for j in range(half):
        width = found[j].shape[1] // 2
        mine, theirs = found[j][:, :width], found[j][:, width:]
        change[0, j] = mine
        change[1, j] = theirs
        stacked[j, member] = dot(mine, moves[j][0])
        stacked[j, 1 - member] = dot(theirs, moves[j][1])


def parent_step(parent, stacked, start, change, grid, made, turned, stored):
    rank = start.shape[0]
    half = parent.shape[0]
    rows = [cat([stacked[j, 0], stacked[j, 1]], 0) for j in range(half)]
    left = [fold(dot(wide(rows[j]), tall(parent[j]))) for j in range(half)]
    grams = []
    for j in range(half):
        high, low = halves(rows[j])
        right = cat([cat([high, high], 1), cat([low, low], 1)], 0)
        grams.append(fold(dot_t(wide(left[j]), right)))
    images = images_of(wide(start[...]), grams)
    for pair in range(half // 2):
        store_gram(grid, stored, pair, images[2 * pair : 2 * pair + 2], rank)
    eliminate(grid, made, turned, rank, half // 2)
    found = [pair_rows(made, stored, pair, rank) for pair in range(half // 2)]
    for j in range(half):
        width = found[0].shape[1] // 2
        at = j % 2 * width
        mixed = wide(found[j // 2][:, at : at + width])
        rows = tall(cat([stacked[j, 0], stacked[j, 1]], 0))
        change[j] = fold(dot(mixed, rows)).astype(BF16)


def parted(value, scratch):
    scratch[...] = value.astype(F32)
    count = value.shape[0] // 2
    return cat(
        [scratch[pl.ds(0, count, stride=2), :], scratch[pl.ds(1, count, stride=2), :]], 0
    ).astype(BF16)


def middle_own(
    change, parent_change, bases, blocks, parents, _,
    own_bases, own_half, parent_half, token,
    order, order_parents,
):
    token[...] = jnp.zeros(token.shape, token.dtype)
    half, links = parents.shape[0], blocks.shape[1]
    first = (lax.axis_index("sub") % 2) * half
    for j in range(half):
        rows = change[0, j]
        ordered = parted(rows, order.at[j % 4])
        own_bases[j] = dot_t(rows, bases[first + j]).astype(BF16)
        own_half[j] = dot(ordered, cat([blocks[first + j, c] for c in range(links)], 1)).astype(BF16)
    for j in range(half):
        ordered = parted(parent_change[j], order_parents.at[j % 4])
        parent_half[j] = dot(
            ordered, cat([parents[j, c] for c in range(parents.shape[1])], 1)
        ).astype(BF16)


def middle_other(swapped, bases, blocks, own_bases, _, new_bases, other_half, order):
    half, links = own_bases.shape[0], blocks.shape[1]
    member = lax.axis_index("sub") % 2
    first = (1 - member) * half
    new_bases[pl.ds(member * half, half)] = own_bases[...]
    for j in range(half):
        rows = swapped[1, j]
        ordered = parted(rows, order.at[j % 4])
        new_bases[first + j] = dot_t(rows, bases[first + j]).astype(BF16)
        other_half[j] = dot(
            ordered, cat([blocks[first + j, c] for c in range(links)], 1)
        ).astype(BF16)


def pack(*refs):
    _, *parts, out = refs
    count = parts[0].shape[0]
    for at, part in enumerate(parts):
        out[at * count : at * count + count] = part[...]


def pause(_, token):
    token[...] = jnp.zeros(token.shape, token.dtype)


def couple(middle, partner):
    full = dot_t(middle, partner)
    count = full.shape[0] // 2
    return cat([full[:count], full[count:]], 1)


def write_rows(out, at, order, links, count):
    for m in range(count):
        out[at, :, m * 128 : m * 128 + 128] = order[8 * m : 8 * m + links, :].astype(BF16)


def leaf_couple(boxes, table_in, own_half, other_half, _, *rest):
    held_boxes, (out, token, held, order) = rest[:-4], rest[-4:]
    table = table_in[...]
    count, links = out.shape[0], out.shape[1]
    half, rank = own_half.shape[:2]
    member = lax.axis_index("sub") % 2
    token[...] = jnp.zeros(token.shape, token.dtype)
    size = 2 * held_boxes[0].shape[1]
    for box, source in zip(boxes, held_boxes):
        for at, place in enumerate(box):
            part = source[2 * at : 2 * at + 2]
            held[place * size : place * size + size] = part.reshape((size,) + part.shape[2:])
    for at in range(count):
        own = at < half
        middle = own_half if own else other_half
        j = at % half
        t = (member if own else 1 - member) * half + j
        rows = jnp.where(member == (0 if own else 1), table[:, j : j + 1], table[:, half + j : half + j + 1])
        for c in range(links):
            order[at % 4, pl.ds(c, rank // 2, stride=8), :] = couple(
                middle[j, :, c * 128 : c * 128 + 128], held[rows[c, 0]]
            )
        write_rows(out, t, order.at[at % 4], links, rank // 2)


def parent_couple(table_in, middle, _, *rest):
    near, (out, held, order, done, sems) = rest[:-5], rest[-5:]
    copies = []
    table = table_in[...]
    count, links = out.shape[0], out.shape[1]
    rank = middle.shape[1]
    for m in range(len(near)):
        held[m * count : m * count + count] = near[m][...]
    for p in range(count):
        for c in range(links):
            order[p % 2, pl.ds(c, rank // 2, stride=8), :] = couple(
                middle[p, :, c * 128 : c * 128 + 128], held[table[c, p]]
            )
        write_rows(done, p, order.at[p % 2], links, rank // 2)
        copies.append(pltpu.make_async_copy(done.at[p], out.at[p], sems.at[p]))
        copies[p].start()
    for copy in copies:
        copy.wait()


VMEM = pl.BlockSpec(memory_space=pltpu.VMEM)
ANY = pl.BlockSpec(memory_space=pl.ANY)
HBM = pl.BlockSpec(memory_space=pltpu.HBM)


def call(body, ins, out_shapes, scratch, name, mib, flops, moved, out_specs=None):
    many = isinstance(out_shapes, list)
    return pl.pallas_call(
        body,
        out_shape=out_shapes,
        in_specs=ins,
        out_specs=out_specs or ([VMEM] * len(out_shapes) if many else VMEM),
        scratch_shapes=scratch,
        name=name,
        compiler_params=pltpu.CompilerParams(vmem_limit_bytes=mib * MIB),
        cost_estimate=pl.CostEstimate(flops=flops, bytes_accessed=moved, transcendentals=0),
    )


def swap(block, axis, mask):
    count = lax.axis_size(axis)
    return lax.ppermute(block, axis, [(i, i ^ mask) for i in range(count)])


def group_order(groups):
    return (0, 2, 3, 1) if groups == 4 else tuple(range(groups))


def shards(
    leaf_bases,
    leaf_transfers,
    leaf_blocks,
    leaf_partner_dev,
    leaf_partner_slot,
    parent_blocks,
    parent_partner_group,
    parent_partner_slot,
    leaf_start,
    parent_start,
):
    count, links, old = leaf_blocks.shape[:3]
    half, parent_links = parent_blocks.shape[:2]
    rank = leaf_start.shape[0]
    points = leaf_bases.shape[1]
    chips = lax.axis_size("sub") // 2
    groups = lax.axis_size("grp")
    shape = jax.ShapeDtypeStruct
    dma = pltpu.SemaphoreType.DMA
    square = half * old * old

    weights = shape((half, old, old), F32)
    other_transfers = swap(leaf_transfers, "sub", 1)
    sent = call(
        sent_weights, [VMEM], weights, [],
        "sent_weights", 8, 2 * links * square * old, 2 * links * square,
    )(leaf_blocks)
    other = swap(sent, "sub", 1)
    order = group_order(groups)
    own, parent_weight, leaf_table, parent_table = call(
        functools.partial(kept_weights, order), [VMEM] * 9,
        [shape((half, rank, old), F32), weights, shape((links, count), jnp.int32), shape((parent_links, half), jnp.int32)],
        [],
        "kept_weights", 8, 2 * (links + parent_links) * square * old, 8 * links * square,
    )(
        leaf_blocks, parent_blocks,
        leaf_partner_dev.T, leaf_partner_slot.T, parent_partner_group.T, parent_partner_slot.T,
        leaf_transfers, leaf_start, other_transfers,
    )
    tables = [
        pltpu.VMEM((8 * rank, 2 * rank), F32),
        pltpu.VMEM((8 * rank, 2 * rank), F32),
        pltpu.VMEM((8 * PANEL, 2 * rank), F32),
        pltpu.VMEM((half, 2 * rank, old), F32),
    ]
    change, stacked = call(
        leaf_step, [VMEM] * 6,
        [shape((2, half, rank, old), BF16), shape((half, 2, rank, old), F32)],
        tables, "leaf_step", 8, 40 * square * old, 8 * square,
    )(own, other, parent_weight, leaf_transfers, other_transfers, leaf_start)

    swapped = swap(change, "sub", 1)
    near = [swap(change, "sub", 2 * m) for m in range(1, chips)]
    parent_change = call(
        parent_step, [VMEM] * 3, shape((half, rank, old), BF16),
        tables, "parent_step", 8, 20 * square * old, 8 * square,
    )(parent_weight, stacked, parent_start)
    parents_held = [parent_change] + [
        swap(parent_change, "grp", m) for m in order[1:]
    ]
    token = shape((8, 128), F32)
    half_shape = shape((half, rank, links * old), BF16)
    own_bases, own_half, parent_half, after_middle = call(
        middle_own, [VMEM] * 6,
        [
            shape((half, rank, points), BF16), half_shape,
            shape((half, rank, parent_links * old), BF16), token,
        ],
        [pltpu.VMEM((4, rank, old), F32), pltpu.VMEM((4, rank, old), F32)],
        "middle_own", 8, 1 << 34, square,
    )(change, parent_change, leaf_bases, leaf_blocks, parent_blocks, swapped)
    packed = call(
        pack, [VMEM] * chips, shape((2 * chips - 2, half, rank, old), BF16), [],
        "pack", 4 + chips, 1 << 34, square,
    )(after_middle, *near)
    new_leaf_bases, other_half = call(
        middle_other, [VMEM] * 5, [shape((count, rank, points), BF16), half_shape],
        [pltpu.VMEM((4, rank, old), F32)],
        "middle_other", 8, square, square,
    )(swapped, leaf_bases, leaf_blocks, own_bases, packed)
    paused = call(pause, [VMEM], token, [], "pause", 4, 1 << 34, square)(packed)
    held = [change, swapped, *near, swap(packed, "sub", 1)]
    boxes = [(0,), (1,)] + [(2 * m,) for m in range(1, chips)]
    boxes += [tuple(2 * m + 1 for m in range(1, chips))]
    new_leaf_blocks, after_leaves = call(
        functools.partial(leaf_couple, boxes), [VMEM] * (4 + len(held)),
        [shape((count, links, rank * rank), BF16), token],
        [
            pltpu.VMEM((2 * chips * count, rank, old), BF16),
            pltpu.VMEM((4, 4 * rank, 2 * rank), F32),
        ],
        "leaf_couple", 4 + chips, 1 << 34, 12 * square,
    )(leaf_table, own_half, other_half, paused, *held)
    new_parent_blocks = call(
        parent_couple, [VMEM] * (groups + 3),
        shape((half, parent_links, rank * rank), BF16),
        [
            pltpu.VMEM((groups * half, rank, old), BF16),
            pltpu.VMEM((2, 4 * rank, 2 * rank), F32),
            pltpu.VMEM((half, parent_links, rank * rank), BF16),
            dma((half,)),
        ],
        "parent_couple", 4 + groups, square, 4 * square, HBM,
    )(parent_table, parent_half, after_leaves, *parents_held)
    return (new_leaf_bases, new_leaf_blocks, new_parent_blocks)


def solution(mesh):
    first = ("grp", "sub")
    placed = (
        P(first, None, None),
        P(first, None, None),
        P(first, None, None, None),
        P(first, None),
        P(first, None),
        P(first, None, None, None),
        P(first, None),
        P(first, None),
        P(),
        P(),
    )
    return jax.shard_map(
        shards,
        mesh=mesh,
        in_specs=placed,
        out_specs=(P(first, None, None),) * 3,
        check_vma=False,
    )
```
